32 devices in a mesh: seq: 4 (over y, x), inner: 8 (over z, core).
Axes of the slice: x: 2, y: 2, z: 4, core: 2. Of those that a mesh axis runs over, the one named last changes fastest.
Arguments:
- queries: bfloat16 [4096, 1024], P('seq', 'inner'), may hold values from -6 to 6
- key_vectors: bfloat16 [4096, 1024], P('seq', 'inner'), may hold values from -6 to 6
- value_vectors: bfloat16 [4096, 1024], P('seq', 'inner'), may hold values from -6 to 6
- out_grad: bfloat16 [4096, 1024], P('seq', 'inner'), may hold values from -6 to 6
Outputs:
- attended: bfloat16 [4096, 1024], P('seq', 'inner')
- query_grad: bfloat16 [4096, 1024], P('seq', 'inner')
- key_grad: bfloat16 [4096, 1024], P('seq', 'inner')
- value_grad: bfloat16 [4096, 1024], P('seq', 'inner')
The draws below stay inside these ranges and needn't reach their ends.
All inputs are finite; a program needn't handle non-finite values.
Results may differ from the reference program's by a relative error of at most 0.0058.
Values sent between devices are 32-bit elements; how exact they have to be, the bound alone decides.
A program may use at most 64 MiB of HBM per device.

```python
import jax
import jax.numpy as jnp
from jax import lax

DK = 128
HEADS = 4
HALF = 1024
BLOCK = 512
TOKENS = 8192
COLS = 512
N_SEQ = 4


def shard_levels(own_key, extent, cuts, smallest, high):
    def one(dim, blocks):
        steps = jax.random.uniform(jax.random.fold_in(jax.random.fold_in(own_key, 6), dim), (blocks,), jnp.float32, smallest / len(cuts), high / len(cuts))
        return jnp.repeat(jnp.exp(steps), extent[dim] // blocks).reshape((-1,) + (1,) * (len(extent) - dim - 1))

    factor_of = one(*cuts[0])
    for cut in cuts[1:]:
        factor_of = factor_of * one(*cut)
    return factor_of


def noise(own_key, shape, deviation, most, cuts=(), kind=jnp.bfloat16):
    factor_of = shard_levels(own_key, shape, cuts, -0.22, 0.18) if cuts else 1.0
    drawn = jax.random.normal(own_key, shape, jnp.float32) * deviation * factor_of
    return jnp.minimum(jnp.maximum(drawn, -most), most).astype(kind)


def setup_inputs(seed: int = 0) -> dict:
    seeds = jax.random.split(jax.random.key(seed), 5)
    return {
        "queries": noise(seeds[0], (TOKENS // 2, 2 * COLS), 1.0, 6.0, ((0, 4), (1, 8))),
        "key_vectors": noise(seeds[1], (TOKENS // 2, 2 * COLS), 1.0, 6.0, ((0, 4), (1, 8))),
        "value_vectors": noise(seeds[2], (TOKENS // 2, 2 * COLS), 1.0, 6.0, ((0, 4), (1, 8))),
        "out_grad": noise(seeds[3], (TOKENS // 2, 2 * COLS), 1.0, 6.0, ((0, 4), (1, 8))),
    }


def from_layout(array):
    shaped = array.reshape(N_SEQ, HALF, HEADS, 2, DK)
    shaped = jnp.transpose(shaped, (0, 3, 1, 2, 4))
    return shaped.reshape(TOKENS, HEADS * DK)

def to_layout(array):
    shaped = array.reshape(N_SEQ, 2, HALF, HEADS, DK)
    shaped = jnp.transpose(shaped, (0, 2, 3, 1, 4))
    return shaped.reshape(TOKENS // 2, 2 * HEADS * DK)

def heads_blocks(array):
    shaped = from_layout(array).reshape(TOKENS // BLOCK, BLOCK, HEADS, DK)
    return jnp.transpose(shaped, (0, 2, 1, 3))

def unblock(array):
    return to_layout(jnp.transpose(array, (0, 2, 1, 3)).reshape(TOKENS, HEADS * DK))

def rounded(values_f):
    return lax.optimization_barrier(values_f.astype(jnp.bfloat16)).astype(jnp.float32)

def prepare(block_index, query_b, key_b, value_b, grad_b):
    row_ids = jnp.arange(BLOCK, dtype=jnp.int32)
    causal = row_ids[:, None] >= row_ids[None, :]
    position = (block_index * BLOCK + row_ids).astype(jnp.float32)
    scaling = 1.0 / jnp.sqrt(DK * (position + 1.0))
    query_f = query_b.astype(jnp.float32)
    key_f = key_b.astype(jnp.float32)
    value_f = value_b.astype(jnp.float32)
    scaled_grad = rounded(scaling[None, :, None] * grad_b.astype(jnp.float32))
    scores = jnp.einsum('hbd,hcd->hbc', query_f, key_f)
    weights = rounded(jnp.where(causal[None], scores, 0.0))
    grad_scores = rounded(jnp.where(causal[None], jnp.einsum('hbv,hcv->hbc', scaled_grad, value_f), 0.0))
    return (scaling, query_f, key_f, value_f, scaled_grad, weights, grad_scores)

def reference(queries, key_vectors, value_vectors, out_grad):
    block_ids = jnp.arange(TOKENS // BLOCK, dtype=jnp.int32)
    inputs = (block_ids, heads_blocks(queries), heads_blocks(key_vectors), heads_blocks(value_vectors), heads_blocks(out_grad))
    zero_state = jnp.zeros((HEADS, DK, DK), jnp.float32)

    def forward(kv_state, pieces):
        scaling, query_f, key_f, value_f, scaled_grad, weights, grad_scores = prepare(*pieces)
        kv_used = rounded(kv_state)
        local = jnp.einsum('hbc,hcv->hbv', weights, value_f)
        carried = jnp.einsum('hbd,hdv->hbv', query_f, kv_used)
        attended = ((local + carried) * scaling[None, :, None]).astype(jnp.bfloat16)
        query_local = jnp.einsum('hbc,hcd->hbd', grad_scores, key_f)
        query_carried = jnp.einsum('hbv,hdv->hbd', scaled_grad, kv_used)
        query_grad = (query_local + query_carried).astype(jnp.bfloat16)
        kv_state = kv_state + jnp.einsum('hcd,hcv->hdv', key_f, value_f)
        return (kv_state, (attended, query_grad))

    def backward(back_state, pieces):
        scaling, query_f, key_f, value_f, scaled_grad, weights, grad_scores = prepare(*pieces)
        back_used = rounded(back_state)
        key_local = jnp.einsum('hbc,hbd->hcd', grad_scores, query_f)
        key_carried = jnp.einsum('hcv,hdv->hcd', value_f, back_used)
        key_grad = (key_local + key_carried).astype(jnp.bfloat16)
        value_local = jnp.einsum('hbc,hbv->hcv', weights, scaled_grad)
        value_carried = jnp.einsum('hcd,hdv->hcv', key_f, back_used)
        value_grad = (value_local + value_carried).astype(jnp.bfloat16)
        back_state = back_state + jnp.einsum('hbd,hbv->hdv', query_f, scaled_grad)
        return (back_state, (key_grad, value_grad))
    final_state, forward_out = lax.scan(forward, zero_state, inputs)
    final_back, backward_out = lax.scan(backward, zero_state, inputs, reverse=True)
    return (unblock(forward_out[0]), unblock(forward_out[1]), unblock(backward_out[0]), unblock(backward_out[1]))
```

```python
import functools

import jax
import jax.numpy as jnp
from jax import lax
from jax.experimental import pallas as pl
from jax.experimental.pallas import tpu as pltpu
from jax.sharding import PartitionSpec as P

MESH = pl.DeviceIdType.MESH
CHUNK = 256
F32 = jnp.float32
BF16 = jnp.bfloat16


def dot(a, b):
    return lax.dot_general(a, b, (((1,), (0,)), ((), ())), preferred_element_type=F32)


def dot_bt(a, b):
    return lax.dot_general(a, b, (((1,), (1,)), ((), ())), preferred_element_type=F32)


def dot_at(a, b):
    return lax.dot_general(a, b, (((0,), (0,)), ((), ())), preferred_element_type=F32)


def xor(index, mask):
    bit = 1
    out = index
    while bit <= mask:
        if mask & bit:
            out = out + bit - 2 * bit * ((index // bit) % 2)
        bit *= 2
    return out


def kernel(
    n_seq,
    q_hbm, k_hbm, v_hbm, o_hbm,
    att_out, qg_out, kg_out, vg_out,
    q_ref, k_ref, v_ref, o_ref, sg_ref, scale_ref,
    acc, before, after, own, part, mid, got, state,
    in_sem, send_sem, recv_sem,
):
    rows, width = q_ref.shape
    count = rows // CHUNK
    half = width // 2
    seq = lax.axis_index("seq")
    inner = lax.axis_index("inner")
    side = inner % 2
    partner = {"inner": inner + 1 - 2 * side}
    mine = pl.ds(pl.multiple_of(side * half, half), half)
    masks = sorted(range(1, n_seq), key=lambda m: -bin(m).count("1"))

    loads = [
        pltpu.make_async_copy(src, dst, in_sem.at[i])
        for i, (src, dst) in enumerate(
            ((k_hbm, k_ref), (v_hbm, v_ref), (o_hbm, o_ref), (q_hbm, q_ref))
        )
    ]
    for load in loads:
        load.start()

    barrier = pltpu.get_barrier_semaphore()
    pl.semaphore_signal(barrier, inc=1, device_id=partner, device_id_type=MESH)
    for mask in masks:
        pl.semaphore_signal(
            barrier, inc=1, device_id={"seq": xor(seq, mask)}, device_id_type=MESH
        )

    def chunk(c):
        return pl.ds(c * CHUNK, CHUNK)

    loads[0].wait()
    loads[1].wait()
    total = None
    for c in range(count):
        outer = dot_at(k_ref[chunk(c), :], v_ref[chunk(c), :])
        if c:
            before[c] = total
        total = outer if total is None else total + outer
    own[0] = total
    pl.semaphore_wait(barrier, n_seq)
    to_partner = [
        pltpu.make_async_remote_copy(
            own.at[i], part.at[i], send_sem.at[i], recv_sem.at[i],
            device_id=partner, device_id_type=MESH,
        )
        for i in range(2)
    ]
    to_partner[0].start()

    loads[2].wait()
    loads[3].wait()
    base = (seq * 2 + side) * rows
    total = None
    for c in reversed(range(count)):
        place = lax.broadcasted_iota(jnp.int32, (CHUNK, width), 0) + (base + c * CHUNK)
        scale = lax.rsqrt(width * (place.astype(F32) + 1.0))
        scale_ref[chunk(c), :] = scale
        scaled = (scale * o_ref[chunk(c), :].astype(F32)).astype(BF16)
        sg_ref[chunk(c), :] = scaled
        outer = dot_at(q_ref[chunk(c), :], scaled)
        if c < count - 1:
            after[c] = total
        total = outer if total is None else total + outer
    own[1] = total
    to_partner[1].start()

    causal = lax.broadcasted_iota(jnp.int32, (CHUNK, CHUNK), 0) >= lax.broadcasted_iota(
        jnp.int32, (CHUNK, CHUNK), 1
    )

    def local(c):
        query, key = q_ref[chunk(c), :], k_ref[chunk(c), :]
        value, grad = v_ref[chunk(c), :], sg_ref[chunk(c), :]
        weights = jnp.where(causal, dot_bt(query, key), 0.0).astype(BF16)
        grad_scores = jnp.where(causal, dot_bt(grad, value), 0.0).astype(BF16)
        acc[0, chunk(c), :] = dot(weights, value)
        acc[1, chunk(c), :] = dot(grad_scores, key)
        acc[2, chunk(c), :] = dot_at(grad_scores, query)
        acc[3, chunk(c), :] = dot_at(weights, grad)

    local(0)

    for i in range(2):
        to_partner[i].wait_recv()
        mid[i] = own[i, mine, :] + part[i, mine, :]
    to_peers = []
    for i, mask in enumerate(masks):
        later = (seq // (1 << (mask.bit_length() - 1))) % 2
        copy = pltpu.make_async_remote_copy(
            mid.at[later], got.at[i], send_sem.at[2 + i], recv_sem.at[2 + i],
            device_id={"seq": xor(seq, mask)}, device_id_type=MESH,
        )
        copy.start()
        to_peers.append((mask, copy))

    for c in range(1, count):
        local(c)

    earlier_sum = jnp.zeros((half, width), F32)
    later_sum = jnp.zeros((half, width), F32)
    for i in reversed(range(len(masks))):
        mask, copy = to_peers[i]
        copy.wait_recv()
        later = (seq // (1 << (mask.bit_length() - 1))) % 2
        block = got[i]
        earlier_sum += jnp.where(later == 1, block, 0.0)
        later_sum += jnp.where(later == 1, 0.0, block)
    state[0, mine, :] = earlier_sum
    state[1, mine, :] = later_sum
    halves = pltpu.make_async_remote_copy(
        state.at[:, mine, :], state.at[:, mine, :],
        send_sem.at[1 + n_seq], recv_sem.at[1 + n_seq],
        device_id=partner, device_id_type=MESH,
    )
    halves.start()
    halves.wait_recv()

    state_in = state[0] + jnp.where(side == 1, part[0], 0.0)
    back_in = state[1] + jnp.where(side == 1, 0.0, part[1])
    for c in range(count):
        kv_used = (state_in + before[c] if c else state_in).astype(BF16)
        back_used = (back_in + after[c] if c < count - 1 else back_in).astype(BF16)
        query, key = q_ref[chunk(c), :], k_ref[chunk(c), :]
        value, grad = v_ref[chunk(c), :], sg_ref[chunk(c), :]
        att_out[chunk(c), :] = (
            scale_ref[chunk(c), :] * (acc[0, chunk(c), :] + dot(query, kv_used))
        ).astype(BF16)
        qg_out[chunk(c), :] = (acc[1, chunk(c), :] + dot_bt(grad, kv_used)).astype(BF16)
        kg_out[chunk(c), :] = (acc[2, chunk(c), :] + dot_bt(value, back_used)).astype(BF16)
        vg_out[chunk(c), :] = (acc[3, chunk(c), :] + dot(key, back_used)).astype(BF16)

    for copy in to_partner:
        copy.wait_send()
    for _, copy in to_peers:
        copy.wait_send()
    halves.wait_send()


def per_device(n_seq, queries, key_vectors, value_vectors, out_grad):
    rows, width = queries.shape
    count = rows // CHUNK
    n_sem = n_seq + 2
    return pl.pallas_call(
        functools.partial(kernel, n_seq),
        out_shape=[jax.ShapeDtypeStruct((rows, width), BF16)] * 4,
        in_specs=[pl.BlockSpec(memory_space=pltpu.HBM)] * 4,
        out_specs=[pl.BlockSpec(memory_space=pltpu.VMEM)] * 4,
        scratch_shapes=[
            pltpu.VMEM((rows, width), BF16),
            pltpu.VMEM((rows, width), BF16),
            pltpu.VMEM((rows, width), BF16),
            pltpu.VMEM((rows, width), BF16),
            pltpu.VMEM((rows, width), BF16),
            pltpu.VMEM((rows, width), F32),
            pltpu.VMEM((4, rows, width), F32),
            pltpu.VMEM((count, width, width), F32),
            pltpu.VMEM((count, width, width), F32),
            pltpu.VMEM((2, width, width), F32),
            pltpu.VMEM((2, width, width), F32),
            pltpu.VMEM((2, width // 2, width), F32),
            pltpu.VMEM((n_seq - 1, width // 2, width), F32),
            pltpu.VMEM((2, width, width), F32),
            pltpu.SemaphoreType.DMA((4,)),
            pltpu.SemaphoreType.DMA((n_sem,)),
            pltpu.SemaphoreType.DMA((n_sem,)),
        ],
        compiler_params=pltpu.CompilerParams(
            collective_id=0, has_side_effects=True, vmem_limit_bytes=24 * 2**20
        ),
        name="linear_attention",
    )(queries, key_vectors, value_vectors, out_grad)


def solution(mesh):
    spec = P("seq", "inner")
    return jax.shard_map(
        functools.partial(per_device, mesh.shape["seq"]),
        mesh=mesh,
        in_specs=(spec,) * 4,
        out_specs=(spec,) * 4,
        check_vma=False,
    )
```

```python
import functools

import jax
import jax.numpy as jnp
from jax import lax
from jax.experimental import pallas as pl
from jax.experimental.pallas import tpu as pltpu
from jax.sharding import PartitionSpec as P

MESH = pl.DeviceIdType.MESH
CHUNK = 256
F32 = jnp.float32
BF16 = jnp.bfloat16


def dot(a, b):
    return lax.dot_general(a, b, (((1,), (0,)), ((), ())), preferred_element_type=F32)


def dot_bt(a, b):
    return lax.dot_general(a, b, (((1,), (1,)), ((), ())), preferred_element_type=F32)


def dot_at(a, b):
    return lax.dot_general(a, b, (((0,), (0,)), ((), ())), preferred_element_type=F32)


def xor(index, mask):
    bit = 1
    out = index
    while bit <= mask:
        if mask & bit:
            out = out + bit - 2 * bit * ((index // bit) % 2)
        bit *= 2
    return out


def exchange_kernel(
    n_seq,
    q_hbm, k_hbm, v_hbm, o_hbm,
    q_ref, k_ref, v_ref, sg_ref, scale_ref, acc, before, after, entering,
    o_ref, own, part, mid, got, state,
    in_sem, send_sem, recv_sem,
):
    rows, width = q_ref.shape
    count = rows // CHUNK
    half = width // 2
    seq = lax.axis_index("seq")
    inner = lax.axis_index("inner")
    side = inner % 2
    partner = {"inner": inner + 1 - 2 * side}
    mine = pl.ds(pl.multiple_of(side * half, half), half)
    masks = sorted(range(1, n_seq), key=lambda m: -bin(m).count("1"))

    loads = [
        pltpu.make_async_copy(src, dst, in_sem.at[i])
        for i, (src, dst) in enumerate(
            ((k_hbm, k_ref), (v_hbm, v_ref), (o_hbm, o_ref), (q_hbm, q_ref))
        )
    ]
    for load in loads:
        load.start()

    barrier = pltpu.get_barrier_semaphore()
    pl.semaphore_signal(barrier, inc=1, device_id=partner, device_id_type=MESH)
    for mask in masks:
        pl.semaphore_signal(
            barrier, inc=1, device_id={"seq": xor(seq, mask)}, device_id_type=MESH
        )

    def chunk(c):
        return pl.ds(c * CHUNK, CHUNK)

    loads[0].wait()
    loads[1].wait()
    total = None
    for c in range(count):
        outer = dot_at(k_ref[chunk(c), :], v_ref[chunk(c), :])
        before[c] = jnp.zeros_like(outer) if total is None else total
        total = outer if total is None else total + outer
    own[0] = total
    pl.semaphore_wait(barrier, n_seq)
    to_partner = [
        pltpu.make_async_remote_copy(
            own.at[i], part.at[i], send_sem.at[i], recv_sem.at[i],
            device_id=partner, device_id_type=MESH,
        )
        for i in range(2)
    ]
    to_partner[0].start()

    loads[2].wait()
    loads[3].wait()
    base = (seq * 2 + side) * rows
    total = None
    for c in reversed(range(count)):
        place = lax.broadcasted_iota(jnp.int32, (CHUNK, width), 0) + (base + c * CHUNK)
        scale = lax.rsqrt(width * (place.astype(F32) + 1.0))
        scale_ref[chunk(c), :] = scale
        scaled = (scale * o_ref[chunk(c), :].astype(F32)).astype(BF16)
        sg_ref[chunk(c), :] = scaled
        outer = dot_at(q_ref[chunk(c), :], scaled)
        after[c] = jnp.zeros_like(outer) if total is None else total
        total = outer if total is None else total + outer
    own[1] = total
    to_partner[1].start()

    causal = lax.broadcasted_iota(jnp.int32, (CHUNK, CHUNK), 0) >= lax.broadcasted_iota(
        jnp.int32, (CHUNK, CHUNK), 1
    )

    def local(c):
        query, key = q_ref[chunk(c), :], k_ref[chunk(c), :]
        value, grad = v_ref[chunk(c), :], sg_ref[chunk(c), :]
        weights = jnp.where(causal, dot_bt(query, key), 0.0).astype(BF16)
        grad_scores = jnp.where(causal, dot_bt(grad, value), 0.0).astype(BF16)
        acc[0, chunk(c), :] = dot(weights, value)
        acc[1, chunk(c), :] = dot(grad_scores, key)
        acc[2, chunk(c), :] = dot_at(grad_scores, query)
        acc[3, chunk(c), :] = dot_at(weights, grad)

    local(0)

    for i in range(2):
        to_partner[i].wait_recv()
        mid[i] = own[i, mine, :] + part[i, mine, :]
    to_peers = []
    for i, mask in enumerate(masks):
        later = (seq // (1 << (mask.bit_length() - 1))) % 2
        copy = pltpu.make_async_remote_copy(
            mid.at[later], got.at[i], send_sem.at[2 + i], recv_sem.at[2 + i],
            device_id={"seq": xor(seq, mask)}, device_id_type=MESH,
        )
        copy.start()
        to_peers.append((mask, copy))

    for c in range(1, count):
        local(c)

    earlier_sum = jnp.zeros((half, width), F32)
    later_sum = jnp.zeros((half, width), F32)
    for i in reversed(range(len(masks))):
        mask, copy = to_peers[i]
        copy.wait_recv()
        later = (seq // (1 << (mask.bit_length() - 1))) % 2
        block = got[i]
        earlier_sum += jnp.where(later == 1, block, 0.0)
        later_sum += jnp.where(later == 1, 0.0, block)
    state[0, mine, :] = earlier_sum
    state[1, mine, :] = later_sum
    halves = pltpu.make_async_remote_copy(
        state.at[:, mine, :], state.at[:, mine, :],
        send_sem.at[1 + n_seq], recv_sem.at[1 + n_seq],
        device_id=partner, device_id_type=MESH,
    )
    halves.start()
    halves.wait_recv()

    entering[0] = state[0] + jnp.where(side == 1, part[0], 0.0)
    entering[1] = state[1] + jnp.where(side == 1, 0.0, part[1])

    for copy in to_partner:
        copy.wait_send()
    for _, copy in to_peers:
        copy.wait_send()
    halves.wait_send()


def carried_kernel(
    q_ref, k_ref, v_ref, sg_ref, scale_ref, acc, before, after, entering,
    att_hbm, qg_hbm, kg_hbm, vg_hbm, out_ref, out_sem,
):
    count = q_ref.shape[0] // CHUNK
    stores = []
    for c in range(count):
        rows = pl.ds(c * CHUNK, CHUNK)
        kv_used = (entering[0] + before[c] if c else entering[0]).astype(BF16)
        back_used = (entering[1] + after[c] if c < count - 1 else entering[1]).astype(BF16)
        query, key, value, grad = (x[rows, :] for x in (q_ref, k_ref, v_ref, sg_ref))
        out_ref[0, rows, :] = (
            scale_ref[rows, :] * (acc[0, rows, :] + dot(query, kv_used))
        ).astype(BF16)
        out_ref[1, rows, :] = (acc[1, rows, :] + dot_bt(grad, kv_used)).astype(BF16)
        out_ref[2, rows, :] = (acc[2, rows, :] + dot_bt(value, back_used)).astype(BF16)
        out_ref[3, rows, :] = (acc[3, rows, :] + dot(key, back_used)).astype(BF16)
        for i, dst in enumerate((att_hbm, qg_hbm, kg_hbm, vg_hbm)):
            store = pltpu.make_async_copy(
                out_ref.at[i, rows, :], dst.at[rows, :], out_sem.at[i, c]
            )
            store.start()
            stores.append(store)
    for store in stores:
        store.wait()


def per_device(n_seq, queries, key_vectors, value_vectors, out_grad):
    rows, width = queries.shape
    count = rows // CHUNK
    n_sem = n_seq + 2
    args = [
        pltpu.with_memory_space_constraint(x, pltpu.HBM)
        for x in (queries, key_vectors, value_vectors, out_grad)
    ]
    tokens = pltpu.VMEM((rows, width), BF16)
    held = [
        ((rows, width), BF16),
        ((rows, width), BF16),
        ((rows, width), BF16),
        ((rows, width), BF16),
        ((rows, width), F32),
        ((4, rows, width), F32),
        ((count, width, width), F32),
        ((count, width, width), F32),
        ((2, width, width), F32),
    ]
    in_vmem = pl.BlockSpec(memory_space=pltpu.VMEM)
    in_hbm = pl.BlockSpec(memory_space=pltpu.HBM)
    local = pl.pallas_call(
        functools.partial(exchange_kernel, n_seq),
        out_shape=[pltpu.VMEM(shape, kind) for shape, kind in held],
        in_specs=[in_hbm] * 4,
        out_specs=[in_vmem] * len(held),
        scratch_shapes=[
            tokens,
            pltpu.VMEM((2, width, width), F32),
            pltpu.VMEM((2, width, width), F32),
            pltpu.VMEM((2, width // 2, width), F32),
            pltpu.VMEM((n_seq - 1, width // 2, width), F32),
            pltpu.VMEM((2, width, width), F32),
            pltpu.SemaphoreType.DMA((4,)),
            pltpu.SemaphoreType.DMA((n_sem,)),
            pltpu.SemaphoreType.DMA((n_sem,)),
        ],
        compiler_params=pltpu.CompilerParams(
            collective_id=0, has_side_effects=True, vmem_limit_bytes=24 * 2**20
        ),
        name="exchange",
    )(*args)
    return pl.pallas_call(
        carried_kernel,
        out_shape=[pltpu.HBM((rows, width), BF16)] * 4,
        in_specs=[in_vmem] * len(held),
        out_specs=[in_hbm] * 4,
        scratch_shapes=[
            pltpu.VMEM((4, rows, width), BF16),
            pltpu.SemaphoreType.DMA((4, count)),
        ],
        compiler_params=pltpu.CompilerParams(vmem_limit_bytes=24 * 2**20),
        name="carried",
    )(*(pltpu.with_memory_space_constraint(x, pltpu.VMEM) for x in local))


def solution(mesh):
    spec = P("seq", "inner")
    return jax.shard_map(
        functools.partial(per_device, mesh.shape["seq"]),
        mesh=mesh,
        in_specs=(spec,) * 4,
        out_specs=(spec,) * 4,
        check_vma=False,
    )
```

```python
import functools

import jax
import jax.numpy as jnp
from jax import lax
from jax.experimental import pallas as pl
from jax.experimental.pallas import tpu as pltpu
from jax.sharding import PartitionSpec as P

MESH = pl.DeviceIdType.MESH
CHUNK = 256
F32 = jnp.float32
BF16 = jnp.bfloat16


def dot(a, b):
    return lax.dot_general(a, b, (((1,), (0,)), ((), ())), preferred_element_type=F32)


def dot_bt(a, b):
    return lax.dot_general(a, b, (((1,), (1,)), ((), ())), preferred_element_type=F32)


def dot_at(a, b):
    return lax.dot_general(a, b, (((0,), (0,)), ((), ())), preferred_element_type=F32)


def xor(index, mask):
    bit = 1
    out = index
    while bit <= mask:
        if mask & bit:
            out = out + bit - 2 * bit * ((index // bit) % 2)
        bit *= 2
    return out


def exchange_kernel(
    n_seq,
    q_hbm, k_hbm, v_hbm, o_hbm,
    q_ref, k_ref, v_ref, sg_ref, scale_ref, acc, before, after, entering,
    o_ref, own, part, mid, got, state,
    in_sem, send_sem, recv_sem,
):
    rows, width = q_ref.shape
    count = rows // CHUNK
    half = width // 2
    seq = lax.axis_index("seq")
    inner = lax.axis_index("inner")
    side = inner % 2
    partner = {"inner": inner + 1 - 2 * side}
    mine = pl.ds(pl.multiple_of(side * half, half), half)
    masks = sorted(range(1, n_seq), key=lambda m: -bin(m).count("1"))

    def chunk(c):
        return pl.ds(c * CHUNK, CHUNK)

    def load(src, dst, i, c):
        copy = pltpu.make_async_copy(src.at[chunk(c), :], dst.at[chunk(c), :], in_sem.at[i, c])
        copy.start()
        return copy

    grad_loads = {
        c: (load(o_hbm, o_ref, 0, c), load(q_hbm, q_ref, 1, c)) for c in reversed(range(count))
    }
    key_loads = [(load(k_hbm, k_ref, 2, c), load(v_hbm, v_ref, 3, c)) for c in range(count)]

    barrier = pltpu.get_barrier_semaphore()
    pl.semaphore_signal(barrier, inc=1, device_id=partner, device_id_type=MESH)
    for mask in masks:
        pl.semaphore_signal(
            barrier, inc=1, device_id={"seq": xor(seq, mask)}, device_id_type=MESH
        )

    base = (seq * 2 + side) * rows
    for c in range(count):
        place = lax.broadcasted_iota(jnp.int32, (CHUNK, width), 0) + (base + c * CHUNK)
        scale_ref[chunk(c), :] = lax.rsqrt(width * (place.astype(F32) + 1.0))

    total = None
    for c in reversed(range(count)):
        for copy in grad_loads[c]:
            copy.wait()
        scaled = (scale_ref[chunk(c), :] * o_ref[chunk(c), :].astype(F32)).astype(BF16)
        sg_ref[chunk(c), :] = scaled
        outer = dot_at(q_ref[chunk(c), :], scaled)
        after[c] = jnp.zeros_like(outer) if total is None else total
        total = outer if total is None else total + outer
    own[1] = total
    pl.semaphore_wait(barrier, n_seq)
    to_partner = [
        pltpu.make_async_remote_copy(
            own.at[i], part.at[i], send_sem.at[i], recv_sem.at[i],
            device_id=partner, device_id_type=MESH,
        )
        for i in range(2)
    ]
    to_partner[1].start()

    total = None
    for c in range(count):
        for copy in key_loads[c]:
            copy.wait()
        outer = dot_at(k_ref[chunk(c), :], v_ref[chunk(c), :])
        before[c] = jnp.zeros_like(outer) if total is None else total
        total = outer if total is None else total + outer
    own[0] = total
    to_partner[0].start()

    causal = lax.broadcasted_iota(jnp.int32, (CHUNK, CHUNK), 0) >= lax.broadcasted_iota(
        jnp.int32, (CHUNK, CHUNK), 1
    )

    def local(c):
        query, key = q_ref[chunk(c), :], k_ref[chunk(c), :]
        value, grad = v_ref[chunk(c), :], sg_ref[chunk(c), :]
        weights = jnp.where(causal, dot_bt(query, key), 0.0).astype(BF16)
        grad_scores = jnp.where(causal, dot_bt(grad, value), 0.0).astype(BF16)
        acc[0, chunk(c), :] = dot(weights, value)
        acc[1, chunk(c), :] = dot(grad_scores, key)
        acc[2, chunk(c), :] = dot_at(grad_scores, query)
        acc[3, chunk(c), :] = dot_at(weights, grad)

    to_peers = []
    for i, mask in enumerate(masks):
        later = (seq // (1 << (mask.bit_length() - 1))) % 2
        copy = pltpu.make_async_remote_copy(
            mid.at[later], got.at[i], send_sem.at[2 + i], recv_sem.at[2 + i],
            device_id={"seq": xor(seq, mask)}, device_id_type=MESH,
        )
        to_peers.append((later, copy))
    for kind in (1, 0):
        to_partner[kind].wait_recv()
        mid[kind] = own[kind, mine, :] + part[kind, mine, :]
        for later, copy in to_peers:
            pl.when(later == kind)(copy.start)

    for c in range(count - 1):
        local(c)

    earlier_sum = jnp.zeros((half, width), F32)
    later_sum = jnp.zeros((half, width), F32)
    for i in reversed(range(len(masks))):
        later, copy = to_peers[i]
        copy.wait_recv()
        block = got[i]
        earlier_sum += jnp.where(later == 1, block, 0.0)
        later_sum += jnp.where(later == 1, 0.0, block)
    state[0, mine, :] = earlier_sum
    state[1, mine, :] = later_sum
    halves = pltpu.make_async_remote_copy(
        state.at[:, mine, :], state.at[:, mine, :],
        send_sem.at[1 + n_seq], recv_sem.at[1 + n_seq],
        device_id=partner, device_id_type=MESH,
    )
    halves.start()
    local(count - 1)
    halves.wait_recv()

    entering[0] = state[0] + jnp.where(side == 1, part[0], 0.0)
    entering[1] = state[1] + jnp.where(side == 1, 0.0, part[1])

    for copy in to_partner:
        copy.wait_send()
    for _, copy in to_peers:
        copy.wait_send()
    halves.wait_send()


def carried_kernel(
    q_ref, k_ref, v_ref, sg_ref, scale_ref, acc, before, after, entering,
    att_hbm, qg_hbm, kg_hbm, vg_hbm, out_ref, out_sem,
):
    count = q_ref.shape[0] // CHUNK
    stores = []
    for c in range(count):
        rows = pl.ds(c * CHUNK, CHUNK)
        kv_used = (entering[0] + before[c] if c else entering[0]).astype(BF16)
        back_used = (entering[1] + after[c] if c < count - 1 else entering[1]).astype(BF16)
        query, key, value, grad = (x[rows, :] for x in (q_ref, k_ref, v_ref, sg_ref))
        out_ref[0, rows, :] = (
            scale_ref[rows, :] * (acc[0, rows, :] + dot(query, kv_used))
        ).astype(BF16)
        out_ref[1, rows, :] = (acc[1, rows, :] + dot_bt(grad, kv_used)).astype(BF16)
        out_ref[2, rows, :] = (acc[2, rows, :] + dot_bt(value, back_used)).astype(BF16)
        out_ref[3, rows, :] = (acc[3, rows, :] + dot(key, back_used)).astype(BF16)
        for i, dst in enumerate((att_hbm, qg_hbm, kg_hbm, vg_hbm)):
            store = pltpu.make_async_copy(
                out_ref.at[i, rows, :], dst.at[rows, :], out_sem.at[i, c]
            )
            store.start()
            stores.append(store)
    for store in stores:
        store.wait()


def per_device(n_seq, queries, key_vectors, value_vectors, out_grad):
    rows, width = queries.shape
    count = rows // CHUNK
    n_sem = n_seq + 2
    args = [
        pltpu.with_memory_space_constraint(x, pltpu.HBM)
        for x in (queries, key_vectors, value_vectors, out_grad)
    ]
    tokens = pltpu.VMEM((rows, width), BF16)
    held = [
        ((rows, width), BF16),
        ((rows, width), BF16),
        ((rows, width), BF16),
        ((rows, width), BF16),
        ((rows, width), F32),
        ((4, rows, width), F32),
        ((count, width, width), F32),
        ((count, width, width), F32),
        ((2, width, width), F32),
    ]
    in_vmem = pl.BlockSpec(memory_space=pltpu.VMEM)
    in_hbm = pl.BlockSpec(memory_space=pltpu.HBM)
    local = pl.pallas_call(
        functools.partial(exchange_kernel, n_seq),
        out_shape=[pltpu.VMEM(shape, kind) for shape, kind in held],
        in_specs=[in_hbm] * 4,
        out_specs=[in_vmem] * len(held),
        scratch_shapes=[
            tokens,
            pltpu.VMEM((2, width, width), F32),
            pltpu.VMEM((2, width, width), F32),
            pltpu.VMEM((2, width // 2, width), F32),
            pltpu.VMEM((n_seq - 1, width // 2, width), F32),
            pltpu.VMEM((2, width, width), F32),
            pltpu.SemaphoreType.DMA((4, count)),
            pltpu.SemaphoreType.DMA((n_sem,)),
            pltpu.SemaphoreType.DMA((n_sem,)),
        ],
        compiler_params=pltpu.CompilerParams(
            collective_id=0, has_side_effects=True, vmem_limit_bytes=24 * 2**20
        ),
        name="exchange",
    )(*args)
    return pl.pallas_call(
        carried_kernel,
        out_shape=[pltpu.HBM((rows, width), BF16)] * 4,
        in_specs=[in_vmem] * len(held),
        out_specs=[in_hbm] * 4,
        scratch_shapes=[
            pltpu.VMEM((4, rows, width), BF16),
            pltpu.SemaphoreType.DMA((4, count)),
        ],
        compiler_params=pltpu.CompilerParams(vmem_limit_bytes=24 * 2**20),
        name="carried",
    )(*(pltpu.with_memory_space_constraint(x, pltpu.VMEM) for x in local))


def solution(mesh):
    spec = P("seq", "inner")
    return jax.shard_map(
        functools.partial(per_device, mesh.shape["seq"]),
        mesh=mesh,
        in_specs=(spec,) * 4,
        out_specs=(spec,) * 4,
        check_vma=False,
    )
```

```python
import functools

import jax
import jax.numpy as jnp
from jax import lax
from jax.experimental import pallas as pl
from jax.experimental.pallas import tpu as pltpu
from jax.sharding import PartitionSpec as P

MESH = pl.DeviceIdType.MESH
CHUNK = 256
F32 = jnp.float32
BF16 = jnp.bfloat16


def dot(a, b):
    return lax.dot_general(a, b, (((1,), (0,)), ((), ())), preferred_element_type=F32)


def dot_bt(a, b):
    return lax.dot_general(a, b, (((1,), (1,)), ((), ())), preferred_element_type=F32)


def dot_at(a, b):
    return lax.dot_general(a, b, (((0,), (0,)), ((), ())), preferred_element_type=F32)


def xor(index, mask):
    bit = 1
    out = index
    while bit <= mask:
        if mask & bit:
            out = out + bit - 2 * bit * ((index // bit) % 2)
        bit *= 2
    return out


def exchange_kernel(
    n_seq,
    q_hbm, k_hbm, v_hbm, o_hbm,
    q_ref, k_ref, v_ref, sg_ref, scale_ref, acc, before, after, entering,
    o_ref, own, part, mid, got, ship, land,
    in_sem, send_sem, recv_sem,
):
    rows, width = q_ref.shape
    count = rows // CHUNK
    seq = lax.axis_index("seq")
    side = lax.axis_index("inner") % 2
    partner = {"inner": lax.axis_index("inner") + 1 - 2 * side}
    masks = sorted(range(1, n_seq), key=lambda m: -bin(m).count("1"))

    loads = [
        pltpu.make_async_copy(src, dst, in_sem.at[i])
        for i, (src, dst) in enumerate(
            ((o_hbm, o_ref), (q_hbm, q_ref), (k_hbm, k_ref), (v_hbm, v_ref))
        )
    ]
    for load in loads:
        load.start()

    barrier = pltpu.get_barrier_semaphore()
    pl.semaphore_signal(barrier, inc=1, device_id=partner, device_id_type=MESH)
    for mask in masks:
        pl.semaphore_signal(
            barrier, inc=1, device_id={"seq": xor(seq, mask)}, device_id_type=MESH
        )

    def chunk(c):
        return pl.ds(c * CHUNK, CHUNK)

    to_partner = pltpu.make_async_remote_copy(
        own.at[1 - side], part, send_sem.at[0], recv_sem.at[0],
        device_id=partner, device_id_type=MESH,
    )
    to_peers = []
    for i, mask in enumerate(masks):
        earlier = (seq // (1 << (mask.bit_length() - 1))) % 2
        copy = pltpu.make_async_remote_copy(
            mid, got.at[i], send_sem.at[2 + i], recv_sem.at[2 + i],
            device_id={"seq": xor(seq, mask)}, device_id_type=MESH,
        )
        to_peers.append((earlier, copy))
    finished = pltpu.make_async_remote_copy(
        ship, land, send_sem.at[1], recv_sem.at[1],
        device_id=partner, device_id_type=MESH,
    )

    base = (seq * 2 + side) * rows
    for c in range(count):
        place = lax.broadcasted_iota(jnp.int32, (CHUNK, width), 0) + (base + c * CHUNK)
        scale_ref[chunk(c), :] = lax.rsqrt(width * (place.astype(F32) + 1.0))

    loads[0].wait()
    loads[1].wait()
    total = None
    for c in reversed(range(count)):
        scaled = (scale_ref[chunk(c), :] * o_ref[chunk(c), :].astype(F32)).astype(BF16)
        sg_ref[chunk(c), :] = scaled
        outer = dot_at(q_ref[chunk(c), :], scaled)
        after[c] = jnp.zeros_like(outer) if total is None else total
        total = outer if total is None else total + outer
    own[1] = total
    pl.semaphore_wait(barrier, n_seq)
    pl.when(side == 0)(to_partner.start)

    loads[2].wait()
    loads[3].wait()
    total = None
    for c in range(count):
        outer = dot_at(k_ref[chunk(c), :], v_ref[chunk(c), :])
        before[c] = jnp.zeros_like(outer) if total is None else total
        total = outer if total is None else total + outer
    own[0] = total
    pl.when(side == 1)(to_partner.start)

    causal = lax.broadcasted_iota(jnp.int32, (CHUNK, CHUNK), 0) >= lax.broadcasted_iota(
        jnp.int32, (CHUNK, CHUNK), 1
    )

    def local(c):
        query, key = q_ref[chunk(c), :], k_ref[chunk(c), :]
        value, grad = v_ref[chunk(c), :], sg_ref[chunk(c), :]
        weights = jnp.where(causal, dot_bt(query, key), 0.0).astype(BF16)
        grad_scores = jnp.where(causal, dot_bt(grad, value), 0.0).astype(BF16)
        acc[0, chunk(c), :] = dot(weights, value)
        acc[1, chunk(c), :] = dot(grad_scores, key)
        acc[2, chunk(c), :] = dot_at(grad_scores, query)
        acc[3, chunk(c), :] = dot_at(weights, grad)

    def send_sum(kind):
        to_partner.wait_recv()
        mid[...] = own[kind] + part[...]
        for earlier, copy in to_peers:
            pl.when(earlier == kind)(copy.start)

    pl.when(side == 1)(lambda: send_sum(1))
    local(0)
    pl.when(side == 0)(lambda: send_sum(0))
    for c in range(1, count):
        local(c)

    entering[side] = jnp.zeros((width, width), F32)
    for i in reversed(range(len(to_peers))):
        earlier, copy = to_peers[i]

        @pl.when(earlier != side)
        def _():
            copy.wait_recv()
            entering[side] += got[i]

    ship[...] = entering[side] + own[side]
    finished.start()
    finished.wait_recv()
    entering[1 - side] = land[...]

    to_partner.wait_send()
    for earlier, copy in to_peers:
        pl.when(earlier == side)(copy.wait_send)
    finished.wait_send()


def carried_kernel(
    q_ref, k_ref, v_ref, sg_ref, scale_ref, acc, before, after, entering,
    att_hbm, qg_hbm, kg_hbm, vg_hbm, out_ref, out_sem,
):
    count = q_ref.shape[0] // CHUNK
    stores = []
    for c in range(count):
        rows = pl.ds(c * CHUNK, CHUNK)
        kv_used = (entering[0] + before[c] if c else entering[0]).astype(BF16)
        back_used = (entering[1] + after[c] if c < count - 1 else entering[1]).astype(BF16)
        query, key, value, grad = (x[rows, :] for x in (q_ref, k_ref, v_ref, sg_ref))
        out_ref[0, rows, :] = (
            scale_ref[rows, :] * (acc[0, rows, :] + dot(query, kv_used))
        ).astype(BF16)
        out_ref[1, rows, :] = (acc[1, rows, :] + dot_bt(grad, kv_used)).astype(BF16)
        out_ref[2, rows, :] = (acc[2, rows, :] + dot_bt(value, back_used)).astype(BF16)
        out_ref[3, rows, :] = (acc[3, rows, :] + dot(key, back_used)).astype(BF16)
        for i, dst in enumerate((att_hbm, qg_hbm, kg_hbm, vg_hbm)):
            store = pltpu.make_async_copy(
                out_ref.at[i, rows, :], dst.at[rows, :], out_sem.at[i, c]
            )
            store.start()
            stores.append(store)
    for store in stores:
        store.wait()


def per_device(n_seq, queries, key_vectors, value_vectors, out_grad):
    rows, width = queries.shape
    count = rows // CHUNK
    n_sem = n_seq + 1
    args = [
        pltpu.with_memory_space_constraint(x, pltpu.HBM)
        for x in (queries, key_vectors, value_vectors, out_grad)
    ]
    tokens = pltpu.VMEM((rows, width), BF16)
    held = [
        ((rows, width), BF16),
        ((rows, width), BF16),
        ((rows, width), BF16),
        ((rows, width), BF16),
        ((rows, width), F32),
        ((4, rows, width), F32),
        ((count, width, width), F32),
        ((count, width, width), F32),
        ((2, width, width), F32),
    ]
    in_vmem = pl.BlockSpec(memory_space=pltpu.VMEM)
    in_hbm = pl.BlockSpec(memory_space=pltpu.HBM)
    local = pl.pallas_call(
        functools.partial(exchange_kernel, n_seq),
        out_shape=[pltpu.VMEM(shape, kind) for shape, kind in held],
        in_specs=[in_hbm] * 4,
        out_specs=[in_vmem] * len(held),
        scratch_shapes=[
            tokens,
            pltpu.VMEM((2, width, width), F32),
            pltpu.VMEM((width, width), F32),
            pltpu.VMEM((width, width), F32),
            pltpu.VMEM((n_seq - 1, width, width), F32),
            pltpu.VMEM((width, width), F32),
            pltpu.VMEM((width, width), F32),
            pltpu.SemaphoreType.DMA((4,)),
            pltpu.SemaphoreType.DMA((n_sem,)),
            pltpu.SemaphoreType.DMA((n_sem,)),
        ],
        compiler_params=pltpu.CompilerParams(
            collective_id=0, has_side_effects=True, vmem_limit_bytes=24 * 2**20
        ),
        name="exchange",
    )(*args)
    return pl.pallas_call(
        carried_kernel,
        out_shape=[pltpu.HBM((rows, width), BF16)] * 4,
        in_specs=[in_vmem] * len(held),
        out_specs=[in_hbm] * 4,
        scratch_shapes=[
            pltpu.VMEM((4, rows, width), BF16),
            pltpu.SemaphoreType.DMA((4, count)),
        ],
        compiler_params=pltpu.CompilerParams(vmem_limit_bytes=24 * 2**20),
        name="carried",
    )(*(pltpu.with_memory_space_constraint(x, pltpu.VMEM) for x in local))


def solution(mesh):
    spec = P("seq", "inner")
    return jax.shard_map(
        functools.partial(per_device, mesh.shape["seq"]),
        mesh=mesh,
        in_specs=(spec,) * 4,
        out_specs=(spec,) * 4,
        check_vma=False,
    )
```

```python
import functools

import jax
import jax.numpy as jnp
from jax import lax
from jax.experimental import pallas as pl
from jax.experimental.pallas import tpu as pltpu
from jax.sharding import PartitionSpec as P

MESH = pl.DeviceIdType.MESH
CHUNK = 256
F32 = jnp.float32
BF16 = jnp.bfloat16


def dot(a, b):
    return lax.dot_general(a, b, (((1,), (0,)), ((), ())), preferred_element_type=F32)


def dot_bt(a, b):
    return lax.dot_general(a, b, (((1,), (1,)), ((), ())), preferred_element_type=F32)


def dot_at(a, b):
    return lax.dot_general(a, b, (((0,), (0,)), ((), ())), preferred_element_type=F32)


def xor(index, mask):
    bit = 1
    out = index
    while bit <= mask:
        if mask & bit:
            out = out + bit - 2 * bit * ((index // bit) % 2)
        bit *= 2
    return out


def exchange_kernel(
    n_seq,
    q_hbm, k_hbm, v_hbm, o_hbm,
    q_ref, k_ref, v_ref, sg_ref, scale_ref, acc, before, after, entering,
    o_ref, own, part, mid, got, ship, land,
    in_sem, send_sem, recv_sem,
):
    rows, width = q_ref.shape
    count = rows // CHUNK
    seq = lax.axis_index("seq")
    side = lax.axis_index("inner") % 2
    partner = {"inner": lax.axis_index("inner") + 1 - 2 * side}
    masks = sorted(range(1, n_seq), key=lambda m: -bin(m).count("1"))

    loads = [
        pltpu.make_async_copy(src, dst, in_sem.at[i])
        for i, (src, dst) in enumerate(
            ((o_hbm, o_ref), (q_hbm, q_ref), (k_hbm, k_ref), (v_hbm, v_ref))
        )
    ]
    for load in loads:
        load.start()

    barrier = pltpu.get_barrier_semaphore()
    pl.semaphore_signal(barrier, inc=1, device_id=partner, device_id_type=MESH)
    for mask in masks:
        pl.semaphore_signal(
            barrier, inc=1, device_id={"seq": xor(seq, mask)}, device_id_type=MESH
        )

    def chunk(c):
        return pl.ds(c * CHUNK, CHUNK)

    to_partner = pltpu.make_async_remote_copy(
        own.at[1 - side], part, send_sem.at[0], recv_sem.at[0],
        device_id=partner, device_id_type=MESH,
    )
    to_peers = []
    for i, mask in enumerate(masks):
        earlier = (seq // (1 << (mask.bit_length() - 1))) % 2
        copy = pltpu.make_async_remote_copy(
            mid, got.at[i], send_sem.at[2 + i], recv_sem.at[2 + i],
            device_id={"seq": xor(seq, mask)}, device_id_type=MESH,
        )
        to_peers.append((earlier, copy))
    finished = pltpu.make_async_remote_copy(
        ship, land, send_sem.at[1], recv_sem.at[1],
        device_id=partner, device_id_type=MESH,
    )

    base = (seq * 2 + side) * rows
    for c in range(count):
        place = lax.broadcasted_iota(jnp.int32, (CHUNK, width), 0) + (base + c * CHUNK)
        scale_ref[chunk(c), :] = lax.rsqrt(width * (place.astype(F32) + 1.0))

    loads[0].wait()
    loads[1].wait()
    total = None
    for c in reversed(range(count)):
        scaled = (scale_ref[chunk(c), :] * o_ref[chunk(c), :].astype(F32)).astype(BF16)
        sg_ref[chunk(c), :] = scaled
        outer = dot_at(q_ref[chunk(c), :], scaled)
        after[c] = jnp.zeros_like(outer) if total is None else total
        total = outer if total is None else total + outer
    own[1] = total

    @pl.when(seq == n_seq - 1)
    def _():
        pl.semaphore_wait(barrier, n_seq)
        pl.when(side == 0)(to_partner.start)

    loads[2].wait()
    loads[3].wait()
    total = None
    for c in range(count):
        outer = dot_at(k_ref[chunk(c), :], v_ref[chunk(c), :])
        before[c] = jnp.zeros_like(outer) if total is None else total
        total = outer if total is None else total + outer
    own[0] = total

    @pl.when(seq != n_seq - 1)
    def _():
        pl.semaphore_wait(barrier, n_seq)
        pl.when(side == 0)(to_partner.start)

    pl.when(side == 1)(to_partner.start)

    causal = lax.broadcasted_iota(jnp.int32, (CHUNK, CHUNK), 0) >= lax.broadcasted_iota(
        jnp.int32, (CHUNK, CHUNK), 1
    )

    def local(c):
        query, key = q_ref[chunk(c), :], k_ref[chunk(c), :]
        value, grad = v_ref[chunk(c), :], sg_ref[chunk(c), :]
        weights = jnp.where(causal, dot_bt(query, key), 0.0).astype(BF16)
        grad_scores = jnp.where(causal, dot_bt(grad, value), 0.0).astype(BF16)
        acc[0, chunk(c), :] = dot(weights, value)
        acc[1, chunk(c), :] = dot(grad_scores, key)
        acc[2, chunk(c), :] = dot_at(grad_scores, query)
        acc[3, chunk(c), :] = dot_at(weights, grad)

    def send_sum(kind):
        to_partner.wait_recv()
        mid[...] = own[kind] + part[...]
        for earlier, copy in to_peers:
            pl.when(earlier == kind)(copy.start)

    pl.when(side == 1)(lambda: send_sum(1))
    local(0)
    pl.when(side == 0)(lambda: send_sum(0))
    for c in range(1, count):
        local(c)

    entering[side] = jnp.zeros((width, width), F32)
    for i in reversed(range(len(to_peers))):
        earlier, copy = to_peers[i]

        @pl.when(earlier != side)
        def _():
            copy.wait_recv()
            entering[side] += got[i]

    ship[...] = entering[side] + own[side]
    finished.start()
    finished.wait_recv()
    entering[1 - side] = land[...]

    to_partner.wait_send()
    for earlier, copy in to_peers:
        pl.when(earlier == side)(copy.wait_send)
    finished.wait_send()


def carried_kernel(
    q_ref, k_ref, v_ref, sg_ref, scale_ref, acc, before, after, entering,
    att_hbm, qg_hbm, kg_hbm, vg_hbm, out_ref, out_sem,
):
    count = q_ref.shape[0] // CHUNK
    stores = []
    for c in range(count):
        rows = pl.ds(c * CHUNK, CHUNK)
        kv_used = (entering[0] + before[c] if c else entering[0]).astype(BF16)
        back_used = (entering[1] + after[c] if c < count - 1 else entering[1]).astype(BF16)
        query, key, value, grad = (x[rows, :] for x in (q_ref, k_ref, v_ref, sg_ref))
        out_ref[0, rows, :] = (
            scale_ref[rows, :] * (acc[0, rows, :] + dot(query, kv_used))
        ).astype(BF16)
        out_ref[1, rows, :] = (acc[1, rows, :] + dot_bt(grad, kv_used)).astype(BF16)
        out_ref[2, rows, :] = (acc[2, rows, :] + dot_bt(value, back_used)).astype(BF16)
        out_ref[3, rows, :] = (acc[3, rows, :] + dot(key, back_used)).astype(BF16)
        for i, dst in enumerate((att_hbm, qg_hbm, kg_hbm, vg_hbm)):
            store = pltpu.make_async_copy(
                out_ref.at[i, rows, :], dst.at[rows, :], out_sem.at[i, c]
            )
            store.start()
            stores.append(store)
    for store in stores:
        store.wait()


def per_device(n_seq, queries, key_vectors, value_vectors, out_grad):
    rows, width = queries.shape
    count = rows // CHUNK
    n_sem = n_seq + 1
    args = [
        pltpu.with_memory_space_constraint(x, pltpu.HBM)
        for x in (queries, key_vectors, value_vectors, out_grad)
    ]
    tokens = pltpu.VMEM((rows, width), BF16)
    held = [
        ((rows, width), BF16),
        ((rows, width), BF16),
        ((rows, width), BF16),
        ((rows, width), BF16),
        ((rows, width), F32),
        ((4, rows, width), F32),
        ((count, width, width), F32),
        ((count, width, width), F32),
        ((2, width, width), F32),
    ]
    in_vmem = pl.BlockSpec(memory_space=pltpu.VMEM)
    in_hbm = pl.BlockSpec(memory_space=pltpu.HBM)
    local = pl.pallas_call(
        functools.partial(exchange_kernel, n_seq),
        out_shape=[pltpu.VMEM(shape, kind) for shape, kind in held],
        in_specs=[in_hbm] * 4,
        out_specs=[in_vmem] * len(held),
        scratch_shapes=[
            tokens,
            pltpu.VMEM((2, width, width), F32),
            pltpu.VMEM((width, width), F32),
            pltpu.VMEM((width, width), F32),
            pltpu.VMEM((n_seq - 1, width, width), F32),
            pltpu.VMEM((width, width), F32),
            pltpu.VMEM((width, width), F32),
            pltpu.SemaphoreType.DMA((4,)),
            pltpu.SemaphoreType.DMA((n_sem,)),
            pltpu.SemaphoreType.DMA((n_sem,)),
        ],
        compiler_params=pltpu.CompilerParams(
            collective_id=0, has_side_effects=True, vmem_limit_bytes=24 * 2**20
        ),
        name="exchange",
    )(*args)
    return pl.pallas_call(
        carried_kernel,
        out_shape=[pltpu.HBM((rows, width), BF16)] * 4,
        in_specs=[in_vmem] * len(held),
        out_specs=[in_hbm] * 4,
        scratch_shapes=[
            pltpu.VMEM((4, rows, width), BF16),
            pltpu.SemaphoreType.DMA((4, count)),
        ],
        compiler_params=pltpu.CompilerParams(vmem_limit_bytes=24 * 2**20),
        name="carried",
    )(*(pltpu.with_memory_space_constraint(x, pltpu.VMEM) for x in local))


def solution(mesh):
    spec = P("seq", "inner")
    return jax.shard_map(
        functools.partial(per_device, mesh.shape["seq"]),
        mesh=mesh,
        in_specs=(spec,) * 4,
        out_specs=(spec,) * 4,
        check_vma=False,
    )
```

```python
import functools

import jax
import jax.numpy as jnp
from jax import lax
from jax.experimental import pallas as pl
from jax.experimental.pallas import tpu as pltpu
from jax.sharding import PartitionSpec as P

MESH = pl.DeviceIdType.MESH
CHUNK = 256
F32 = jnp.float32
BF16 = jnp.bfloat16


def dot(a, b):
    return lax.dot_general(a, b, (((1,), (0,)), ((), ())), preferred_element_type=F32)


def dot_bt(a, b):
    return lax.dot_general(a, b, (((1,), (1,)), ((), ())), preferred_element_type=F32)


def dot_at(a, b):
    return lax.dot_general(a, b, (((0,), (0,)), ((), ())), preferred_element_type=F32)


def xor(index, mask):
    bit = 1
    out = index
    while bit <= mask:
        if mask & bit:
            out = out + bit - 2 * bit * ((index // bit) % 2)
        bit *= 2
    return out


def exchange_kernel(
    n_seq,
    q_hbm, k_hbm, v_hbm, o_hbm,
    q_ref, k_ref, v_ref, sg_ref, scale_ref, acc, before, after, entering,
    o_ref, own, part, mid, got, ship, land,
    in_sem, send_sem, recv_sem,
):
    rows, width = q_ref.shape
    count = rows // CHUNK
    seq = lax.axis_index("seq")
    side = lax.axis_index("inner") % 2
    partner = {"inner": lax.axis_index("inner") + 1 - 2 * side}
    masks = sorted(range(1, n_seq), key=lambda m: -bin(m).count("1"))

    loads = [
        pltpu.make_async_copy(src, dst, in_sem.at[i])
        for i, (src, dst) in enumerate(
            ((o_hbm, o_ref), (q_hbm, q_ref), (k_hbm, k_ref), (v_hbm, v_ref))
        )
    ]
    for load in loads:
        load.start()

    barrier = pltpu.get_barrier_semaphore()
    pl.semaphore_signal(barrier, inc=1, device_id=partner, device_id_type=MESH)
    for mask in masks:
        pl.semaphore_signal(
            barrier, inc=1, device_id={"seq": xor(seq, mask)}, device_id_type=MESH
        )

    def chunk(c):
        return pl.ds(c * CHUNK, CHUNK)

    to_partner = pltpu.make_async_remote_copy(
        own.at[1 - side], part, send_sem.at[0], recv_sem.at[0],
        device_id=partner, device_id_type=MESH,
    )
    to_peers = []
    for i, mask in enumerate(masks):
        earlier = (seq // (1 << (mask.bit_length() - 1))) % 2
        copy = pltpu.make_async_remote_copy(
            mid, got.at[i], send_sem.at[2 + i], recv_sem.at[2 + i],
            device_id={"seq": xor(seq, mask)}, device_id_type=MESH,
        )
        to_peers.append((earlier, copy))
    finished = pltpu.make_async_remote_copy(
        ship, land, send_sem.at[1], recv_sem.at[1],
        device_id=partner, device_id_type=MESH,
    )

    base = (seq * 2 + side) * rows
    for c in range(count):
        place = lax.broadcasted_iota(jnp.int32, (CHUNK, width), 0) + (base + c * CHUNK)
        scale_ref[chunk(c), :] = lax.rsqrt(width * (place.astype(F32) + 1.0))

    row_ids = lax.broadcasted_iota(jnp.int32, (CHUNK, CHUNK), 0)
    column_ids = lax.broadcasted_iota(jnp.int32, (CHUNK, CHUNK), 1)
    causal, causal_t = row_ids >= column_ids, row_ids <= column_ids

    def local(c):
        query, key = q_ref[chunk(c), :], k_ref[chunk(c), :]
        value, grad = v_ref[chunk(c), :], sg_ref[chunk(c), :]
        weights = jnp.where(causal, dot_bt(query, key), 0.0).astype(BF16)
        acc[0, chunk(c), :] = dot(weights, value)
        grad_scores = jnp.where(causal, dot_bt(grad, value), 0.0).astype(BF16)
        acc[1, chunk(c), :] = dot(grad_scores, key)
        grad_scores_t = jnp.where(causal_t, dot_bt(value, grad), 0.0).astype(BF16)
        acc[2, chunk(c), :] = dot(grad_scores_t, query)
        weights_t = jnp.where(causal_t, dot_bt(key, query), 0.0).astype(BF16)
        acc[3, chunk(c), :] = dot(weights_t, grad)

    loads[0].wait()
    loads[1].wait()
    total = None
    for c in reversed(range(count)):
        scaled = (scale_ref[chunk(c), :] * o_ref[chunk(c), :].astype(F32)).astype(BF16)
        sg_ref[chunk(c), :] = scaled
        outer = dot_at(q_ref[chunk(c), :], scaled)
        after[c] = jnp.zeros_like(outer) if total is None else total
        total = outer if total is None else total + outer
    own[1] = total

    @pl.when(seq == n_seq - 1)
    def _():
        pl.semaphore_wait(barrier, n_seq)
        pl.when(side == 0)(to_partner.start)

    loads[2].wait()
    loads[3].wait()
    total = None
    for c in range(count):
        outer = dot_at(k_ref[chunk(c), :], v_ref[chunk(c), :])
        before[c] = jnp.zeros_like(outer) if total is None else total
        total = outer if total is None else total + outer
    own[0] = total

    ahead = count // 2

    @pl.when(seq == 0)
    def _():
        for c in range(ahead):
            local(c)

    @pl.when(seq != n_seq - 1)
    def _():
        pl.semaphore_wait(barrier, n_seq)
        pl.when(side == 0)(to_partner.start)

    pl.when(side == 1)(to_partner.start)

    def send_sum(kind):
        to_partner.wait_recv()
        mid[...] = own[kind] + part[...]
        for earlier, copy in to_peers:
            pl.when(earlier == kind)(copy.start)

    pl.when(side == 1)(lambda: send_sum(1))

    @pl.when(seq != 0)
    def _():
        local(0)

    pl.when(side == 0)(lambda: send_sum(0))

    @pl.when(seq != 0)
    def _():
        for c in range(1, ahead):
            local(c)

    for c in range(ahead, count):
        local(c)

    entering[side] = jnp.zeros((width, width), F32)
    for i in reversed(range(len(to_peers))):
        earlier, copy = to_peers[i]

        @pl.when(earlier != side)
        def _():
            copy.wait_recv()
            entering[side] += got[i]

    ship[...] = entering[side] + own[side]
    finished.start()
    finished.wait_recv()
    entering[1 - side] = land[...]

    to_partner.wait_send()
    for earlier, copy in to_peers:
        pl.when(earlier == side)(copy.wait_send)
    finished.wait_send()


def carried_kernel(
    q_ref, k_ref, v_ref, sg_ref, scale_ref, acc, before, after, entering,
    att_hbm, qg_hbm, kg_hbm, vg_hbm, out_ref, out_sem,
):
    count = q_ref.shape[0] // CHUNK
    stores = []
    for c in range(count):
        rows = pl.ds(c * CHUNK, CHUNK)
        kv_used = (entering[0] + before[c] if c else entering[0]).astype(BF16)
        back_used = (entering[1] + after[c] if c < count - 1 else entering[1]).astype(BF16)
        query, key, value, grad = (x[rows, :] for x in (q_ref, k_ref, v_ref, sg_ref))
        out_ref[0, rows, :] = (
            scale_ref[rows, :] * (acc[0, rows, :] + dot(query, kv_used))
        ).astype(BF16)
        out_ref[1, rows, :] = (acc[1, rows, :] + dot_bt(grad, kv_used)).astype(BF16)
        out_ref[2, rows, :] = (acc[2, rows, :] + dot_bt(value, back_used)).astype(BF16)
        out_ref[3, rows, :] = (acc[3, rows, :] + dot(key, back_used)).astype(BF16)
        for i, dst in enumerate((att_hbm, qg_hbm, kg_hbm, vg_hbm)):
            store = pltpu.make_async_copy(
                out_ref.at[i, rows, :], dst.at[rows, :], out_sem.at[i, c]
            )
            store.start()
            stores.append(store)
    for store in stores:
        store.wait()


def per_device(n_seq, queries, key_vectors, value_vectors, out_grad):
    rows, width = queries.shape
    count = rows // CHUNK
    n_sem = n_seq + 1
    args = [
        pltpu.with_memory_space_constraint(x, pltpu.HBM)
        for x in (queries, key_vectors, value_vectors, out_grad)
    ]
    tokens = pltpu.VMEM((rows, width), BF16)
    held = [
        ((rows, width), BF16),
        ((rows, width), BF16),
        ((rows, width), BF16),
        ((rows, width), BF16),
        ((rows, width), F32),
        ((4, rows, width), F32),
        ((count, width, width), F32),
        ((count, width, width), F32),
        ((2, width, width), F32),
    ]
    in_vmem = pl.BlockSpec(memory_space=pltpu.VMEM)
    in_hbm = pl.BlockSpec(memory_space=pltpu.HBM)
    local = pl.pallas_call(
        functools.partial(exchange_kernel, n_seq),
        out_shape=[pltpu.VMEM(shape, kind) for shape, kind in held],
        in_specs=[in_hbm] * 4,
        out_specs=[in_vmem] * len(held),
        scratch_shapes=[
            tokens,
            pltpu.VMEM((2, width, width), F32),
            pltpu.VMEM((width, width), F32),
            pltpu.VMEM((width, width), F32),
            pltpu.VMEM((n_seq - 1, width, width), F32),
            pltpu.VMEM((width, width), F32),
            pltpu.VMEM((width, width), F32),
            pltpu.SemaphoreType.DMA((4,)),
            pltpu.SemaphoreType.DMA((n_sem,)),
            pltpu.SemaphoreType.DMA((n_sem,)),
        ],
        compiler_params=pltpu.CompilerParams(
            collective_id=0, has_side_effects=True, vmem_limit_bytes=24 * 2**20
        ),
        name="exchange",
    )(*args)
    return pl.pallas_call(
        carried_kernel,
        out_shape=[pltpu.HBM((rows, width), BF16)] * 4,
        in_specs=[in_vmem] * len(held),
        out_specs=[in_hbm] * 4,
        scratch_shapes=[
            pltpu.VMEM((4, rows, width), BF16),
            pltpu.SemaphoreType.DMA((4, count)),
        ],
        compiler_params=pltpu.CompilerParams(vmem_limit_bytes=24 * 2**20),
        name="carried",
    )(*(pltpu.with_memory_space_constraint(x, pltpu.VMEM) for x in local))


def solution(mesh):
    spec = P("seq", "inner")
    return jax.shard_map(
        functools.partial(per_device, mesh.shape["seq"]),
        mesh=mesh,
        in_specs=(spec,) * 4,
        out_specs=(spec,) * 4,
        check_vma=False,
    )
```

```python
import functools

import jax
import jax.numpy as jnp
from jax import lax
from jax.experimental import pallas as pl
from jax.experimental.pallas import tpu as pltpu
from jax.sharding import PartitionSpec as P

MESH = pl.DeviceIdType.MESH
CHUNK = 256
F32 = jnp.float32
BF16 = jnp.bfloat16


def dot(a, b):
    return lax.dot_general(a, b, (((1,), (0,)), ((), ())), preferred_element_type=F32)


def dot_bt(a, b):
    return lax.dot_general(a, b, (((1,), (1,)), ((), ())), preferred_element_type=F32)


def dot_at(a, b):
    return lax.dot_general(a, b, (((0,), (0,)), ((), ())), preferred_element_type=F32)


def xor(index, mask):
    bit = 1
    out = index
    while bit <= mask:
        if mask & bit:
            out = out + bit - 2 * bit * ((index // bit) % 2)
        bit *= 2
    return out


def exchange_kernel(
    n_seq,
    q_hbm, k_hbm, v_hbm, o_hbm,
    q_ref, k_ref, v_ref, sg_ref, scale_ref, acc, before, after, entering,
    o_ref, own, part, mid, got, ship, land,
    in_sem, send_sem, recv_sem,
):
    rows, width = q_ref.shape
    count = rows // CHUNK
    seq = lax.axis_index("seq")
    side = lax.axis_index("inner") % 2
    partner = {"inner": lax.axis_index("inner") + 1 - 2 * side}
    masks = sorted(range(1, n_seq), key=lambda m: -bin(m).count("1"))

    cut = rows // 2
    loads = [
        [
            pltpu.make_async_copy(
                src.at[pl.ds(p * cut, cut), :], dst.at[pl.ds(p * cut, cut), :], in_sem.at[i, p]
            )
            for p in range(2)
        ]
        for i, (src, dst) in enumerate(
            ((o_hbm, o_ref), (q_hbm, q_ref), (k_hbm, k_ref), (v_hbm, v_ref))
        )
    ]
    for pair in loads:
        for load in pair:
            load.start()

    barrier = pltpu.get_barrier_semaphore()
    pl.semaphore_signal(barrier, inc=1, device_id=partner, device_id_type=MESH)
    for mask in masks:
        pl.semaphore_signal(
            barrier, inc=1, device_id={"seq": xor(seq, mask)}, device_id_type=MESH
        )

    def chunk(c):
        return pl.ds(c * CHUNK, CHUNK)

    owned = 1 - side
    to_partner = pltpu.make_async_remote_copy(
        own.at[side], part, send_sem.at[0], recv_sem.at[0],
        device_id=partner, device_id_type=MESH,
    )
    to_peers = []
    for i, mask in enumerate(masks):
        earlier = (seq // (1 << (mask.bit_length() - 1))) % 2
        copy = pltpu.make_async_remote_copy(
            mid, got.at[i], send_sem.at[2 + i], recv_sem.at[2 + i],
            device_id={"seq": xor(seq, mask)}, device_id_type=MESH,
        )
        to_peers.append((earlier, copy))
    finished = pltpu.make_async_remote_copy(
        ship, land, send_sem.at[1], recv_sem.at[1],
        device_id=partner, device_id_type=MESH,
    )

    base = (seq * 2 + side) * rows
    for c in range(count):
        place = lax.broadcasted_iota(jnp.int32, (CHUNK, width), 0) + (base + c * CHUNK)
        scale_ref[chunk(c), :] = lax.rsqrt(width * (place.astype(F32) + 1.0))

    row_ids = lax.broadcasted_iota(jnp.int32, (CHUNK, CHUNK), 0)
    column_ids = lax.broadcasted_iota(jnp.int32, (CHUNK, CHUNK), 1)
    causal, causal_t = row_ids >= column_ids, row_ids <= column_ids

    def local(c):
        query, key = q_ref[chunk(c), :], k_ref[chunk(c), :]
        value, grad = v_ref[chunk(c), :], sg_ref[chunk(c), :]
        weights = jnp.where(causal, dot_bt(query, key), 0.0).astype(BF16)
        acc[0, chunk(c), :] = dot(weights, value)
        grad_scores = jnp.where(causal, dot_bt(grad, value), 0.0).astype(BF16)
        acc[1, chunk(c), :] = dot(grad_scores, key)
        grad_scores_t = jnp.where(causal_t, dot_bt(value, grad), 0.0).astype(BF16)
        acc[2, chunk(c), :] = dot(grad_scores_t, query)
        weights_t = jnp.where(causal_t, dot_bt(key, query), 0.0).astype(BF16)
        acc[3, chunk(c), :] = dot(weights_t, grad)

    for load in loads[0]:
        load.wait()
    for load in loads[1]:
        load.wait()
    total = None
    for c in reversed(range(count)):
        scaled = (scale_ref[chunk(c), :] * o_ref[chunk(c), :].astype(F32)).astype(BF16)
        sg_ref[chunk(c), :] = scaled
        outer = dot_at(q_ref[chunk(c), :], scaled)
        after[c] = jnp.zeros_like(outer) if total is None else total
        total = outer if total is None else total + outer
    own[1] = total

    @pl.when(seq == n_seq - 1)
    def _():
        pl.semaphore_wait(barrier, n_seq)
        pl.when(side == 1)(to_partner.start)

    for load in loads[2]:
        load.wait()
    for load in loads[3]:
        load.wait()
    total = None
    for c in range(count):
        outer = dot_at(k_ref[chunk(c), :], v_ref[chunk(c), :])
        before[c] = jnp.zeros_like(outer) if total is None else total
        total = outer if total is None else total + outer
    own[0] = total

    ahead = count // 2

    @pl.when(seq == 0)
    def _():
        for c in range(ahead):
            local(c)

    @pl.when(seq != n_seq - 1)
    def _():
        pl.semaphore_wait(barrier, n_seq)
        pl.when(side == 1)(to_partner.start)

    pl.when(side == 0)(to_partner.start)

    def send_sum(kind):
        to_partner.wait_recv()
        mid[...] = own[kind] + part[...]
        for earlier, copy in to_peers:
            pl.when(earlier == kind)(copy.start)

    pl.when(side == 0)(lambda: send_sum(1))

    @pl.when(seq != 0)
    def _():
        local(0)

    pl.when(side == 1)(lambda: send_sum(0))

    @pl.when(seq != 0)
    def _():
        for c in range(1, ahead):
            local(c)

    for c in range(ahead, count):
        local(c)

    ship[...] = jnp.zeros((width, width), F32)
    for i in reversed(range(len(to_peers))):
        earlier, copy = to_peers[i]

        @pl.when(earlier != owned)
        def _():
            copy.wait_recv()
            ship[...] += got[i]

    finished.start()
    entering[owned] = ship[...] + part[...]
    finished.wait_recv()
    entering[side] = land[...]

    to_partner.wait_send()
    for earlier, copy in to_peers:
        pl.when(earlier == owned)(copy.wait_send)
    finished.wait_send()


def carried_kernel(
    q_ref, k_ref, v_ref, sg_ref, scale_ref, acc, before, after, entering,
    att_hbm, qg_hbm, kg_hbm, vg_hbm, out_ref, out_sem,
):
    count = q_ref.shape[0] // CHUNK
    stores = []
    for c in range(count):
        rows = pl.ds(c * CHUNK, CHUNK)
        kv_used = (entering[0] + before[c] if c else entering[0]).astype(BF16)
        back_used = (entering[1] + after[c] if c < count - 1 else entering[1]).astype(BF16)
        query, key, value, grad = (x[rows, :] for x in (q_ref, k_ref, v_ref, sg_ref))
        out_ref[0, rows, :] = (
            scale_ref[rows, :] * (acc[0, rows, :] + dot(query, kv_used))
        ).astype(BF16)
        out_ref[1, rows, :] = (acc[1, rows, :] + dot_bt(grad, kv_used)).astype(BF16)
        out_ref[2, rows, :] = (acc[2, rows, :] + dot_bt(value, back_used)).astype(BF16)
        out_ref[3, rows, :] = (acc[3, rows, :] + dot(key, back_used)).astype(BF16)
        for i, dst in enumerate((att_hbm, qg_hbm, kg_hbm, vg_hbm)):
            store = pltpu.make_async_copy(
                out_ref.at[i, rows, :], dst.at[rows, :], out_sem.at[i, c]
            )
            store.start()
            stores.append(store)
    for store in stores:
        store.wait()


def per_device(n_seq, queries, key_vectors, value_vectors, out_grad):
    rows, width = queries.shape
    count = rows // CHUNK
    n_sem = n_seq + 1
    args = [
        pltpu.with_memory_space_constraint(x, pltpu.HBM)
        for x in (queries, key_vectors, value_vectors, out_grad)
    ]
    tokens = pltpu.VMEM((rows, width), BF16)
    held = [
        ((rows, width), BF16),
        ((rows, width), BF16),
        ((rows, width), BF16),
        ((rows, width), BF16),
        ((rows, width), F32),
        ((4, rows, width), F32),
        ((count, width, width), F32),
        ((count, width, width), F32),
        ((2, width, width), F32),
    ]
    in_vmem = pl.BlockSpec(memory_space=pltpu.VMEM)
    in_hbm = pl.BlockSpec(memory_space=pltpu.HBM)
    local = pl.pallas_call(
        functools.partial(exchange_kernel, n_seq),
        out_shape=[pltpu.VMEM(shape, kind) for shape, kind in held],
        in_specs=[in_hbm] * 4,
        out_specs=[in_vmem] * len(held),
        scratch_shapes=[
            tokens,
            pltpu.VMEM((2, width, width), F32),
            pltpu.VMEM((width, width), F32),
            pltpu.VMEM((width, width), F32),
            pltpu.VMEM((n_seq - 1, width, width), F32),
            pltpu.VMEM((width, width), F32),
            pltpu.VMEM((width, width), F32),
            pltpu.SemaphoreType.DMA((4, 2)),
            pltpu.SemaphoreType.DMA((n_sem,)),
            pltpu.SemaphoreType.DMA((n_sem,)),
        ],
        compiler_params=pltpu.CompilerParams(
            collective_id=0, has_side_effects=True, vmem_limit_bytes=24 * 2**20
        ),
        name="exchange",
    )(*args)
    return pl.pallas_call(
        carried_kernel,
        out_shape=[pltpu.HBM((rows, width), BF16)] * 4,
        in_specs=[in_vmem] * len(held),
        out_specs=[in_hbm] * 4,
        scratch_shapes=[
            pltpu.VMEM((4, rows, width), BF16),
            pltpu.SemaphoreType.DMA((4, count)),
        ],
        compiler_params=pltpu.CompilerParams(vmem_limit_bytes=24 * 2**20),
        name="carried",
    )(*(pltpu.with_memory_space_constraint(x, pltpu.VMEM) for x in local))


def solution(mesh):
    spec = P("seq", "inner")
    return jax.shard_map(
        functools.partial(per_device, mesh.shape["seq"]),
        mesh=mesh,
        in_specs=(spec,) * 4,
        out_specs=(spec,) * 4,
        check_vma=False,
    )
```

```python
import functools

import jax
import jax.numpy as jnp
from jax import lax
from jax.experimental import pallas as pl
from jax.experimental.pallas import tpu as pltpu
from jax.sharding import PartitionSpec as P

MESH = pl.DeviceIdType.MESH
CHUNK = 256
F32 = jnp.float32
BF16 = jnp.bfloat16


def dot(a, b):
    return lax.dot_general(a, b, (((1,), (0,)), ((), ())), preferred_element_type=F32)


def dot_bt(a, b):
    return lax.dot_general(a, b, (((1,), (1,)), ((), ())), preferred_element_type=F32)


def dot_at(a, b):
    return lax.dot_general(a, b, (((0,), (0,)), ((), ())), preferred_element_type=F32)


def xor(index, mask):
    bit = 1
    out = index
    while bit <= mask:
        if mask & bit:
            out = out + bit - 2 * bit * ((index // bit) % 2)
        bit *= 2
    return out


def exchange_kernel(
    n_seq,
    q_hbm, k_hbm, v_hbm, o_hbm,
    q_ref, k_ref, v_ref, sg_ref, scale_ref, acc, before, after, entering,
    o_ref, own, part, mid, got, ship, land,
    in_sem, send_sem, recv_sem,
):
    rows, width = q_ref.shape
    count = rows // CHUNK
    seq = lax.axis_index("seq")
    side = lax.axis_index("inner") % 2
    partner = {"inner": lax.axis_index("inner") + 1 - 2 * side}
    masks = sorted(range(1, n_seq), key=lambda m: -bin(m).count("1"))

    loads = [
        pltpu.make_async_copy(src, dst, in_sem.at[i])
        for i, (src, dst) in enumerate(
            ((o_hbm, o_ref), (q_hbm, q_ref), (k_hbm, k_ref), (v_hbm, v_ref))
        )
    ]
    loads[0].start()
    loads[1].start()

    barrier = pltpu.get_barrier_semaphore()
    pl.semaphore_signal(barrier, inc=1, device_id=partner, device_id_type=MESH)
    for mask in masks:
        pl.semaphore_signal(
            barrier, inc=1, device_id={"seq": xor(seq, mask)}, device_id_type=MESH
        )

    def chunk(c):
        return pl.ds(c * CHUNK, CHUNK)

    owned = 1 - side
    to_partner = pltpu.make_async_remote_copy(
        own.at[side], part, send_sem.at[0], recv_sem.at[0],
        device_id=partner, device_id_type=MESH,
    )
    to_peers = []
    for i, mask in enumerate(masks):
        earlier = (seq // (1 << (mask.bit_length() - 1))) % 2
        copy = pltpu.make_async_remote_copy(
            mid, got.at[i], send_sem.at[2 + i], recv_sem.at[2 + i],
            device_id={"seq": xor(seq, mask)}, device_id_type=MESH,
        )
        to_peers.append((earlier, copy))
    finished = pltpu.make_async_remote_copy(
        ship, land, send_sem.at[1], recv_sem.at[1],
        device_id=partner, device_id_type=MESH,
    )

    base = (seq * 2 + side) * rows
    for c in range(count):
        place = lax.broadcasted_iota(jnp.int32, (CHUNK, width), 0) + (base + c * CHUNK)
        scale_ref[chunk(c), :] = lax.rsqrt(width * (place.astype(F32) + 1.0))

    row_ids = lax.broadcasted_iota(jnp.int32, (CHUNK, CHUNK), 0)
    column_ids = lax.broadcasted_iota(jnp.int32, (CHUNK, CHUNK), 1)
    causal, causal_t = row_ids >= column_ids, row_ids <= column_ids

    def local(c):
        query, key = q_ref[chunk(c), :], k_ref[chunk(c), :]
        value, grad = v_ref[chunk(c), :], sg_ref[chunk(c), :]
        weights = jnp.where(causal, dot_bt(query, key), 0.0).astype(BF16)
        acc[0, chunk(c), :] = dot(weights, value)
        grad_scores = jnp.where(causal, dot_bt(grad, value), 0.0).astype(BF16)
        acc[1, chunk(c), :] = dot(grad_scores, key)
        grad_scores_t = jnp.where(causal_t, dot_bt(value, grad), 0.0).astype(BF16)
        acc[2, chunk(c), :] = dot(grad_scores_t, query)
        weights_t = jnp.where(causal_t, dot_bt(key, query), 0.0).astype(BF16)
        acc[3, chunk(c), :] = dot(weights_t, grad)

    def send_sum(kind):
        to_partner.wait_recv()
        mid[...] = own[kind] + part[...]
        for earlier, copy in to_peers:
            pl.when(earlier == kind)(copy.start)

    loads[0].wait()
    loads[1].wait()
    loads[2].start()
    loads[3].start()
    total = None
    for c in reversed(range(count)):
        scaled = (scale_ref[chunk(c), :] * o_ref[chunk(c), :].astype(F32)).astype(BF16)
        sg_ref[chunk(c), :] = scaled
        outer = dot_at(q_ref[chunk(c), :], scaled)
        after[c] = jnp.zeros_like(outer) if total is None else total
        total = outer if total is None else total + outer
    own[1] = total

    @pl.when(seq == n_seq - 1)
    def _():
        pl.semaphore_wait(barrier, n_seq)
        pl.when(side == 1)(to_partner.start)
        pl.when(side == 0)(lambda: send_sum(1))

    loads[2].wait()
    loads[3].wait()
    total = None
    for c in range(count):
        outer = dot_at(k_ref[chunk(c), :], v_ref[chunk(c), :])
        before[c] = jnp.zeros_like(outer) if total is None else total
        total = outer if total is None else total + outer
    own[0] = total

    ahead = count // 2

    @pl.when(seq == 0)
    def _():
        for c in range(ahead):
            local(c)

    @pl.when(seq != n_seq - 1)
    def _():
        pl.semaphore_wait(barrier, n_seq)
        pl.when(side == 1)(to_partner.start)

    pl.when(side == 0)(to_partner.start)

    pl.when((side == 0) & (seq != n_seq - 1))(lambda: send_sum(1))

    @pl.when(seq != 0)
    def _():
        local(0)

    pl.when(side == 1)(lambda: send_sum(0))

    @pl.when(seq != 0)
    def _():
        for c in range(1, ahead):
            local(c)

    for c in range(ahead, count):
        local(c)

    ship[...] = jnp.zeros((width, width), F32)
    for i in reversed(range(len(to_peers))):
        earlier, copy = to_peers[i]

        @pl.when(earlier != owned)
        def _():
            copy.wait_recv()
            ship[...] += got[i]

    finished.start()
    entering[owned] = ship[...] + part[...]
    finished.wait_recv()
    entering[side] = land[...]

    to_partner.wait_send()
    for earlier, copy in to_peers:
        pl.when(earlier == owned)(copy.wait_send)
    finished.wait_send()


def carried_kernel(
    q_ref, k_ref, v_ref, sg_ref, scale_ref, acc, before, after, entering,
    att_hbm, qg_hbm, kg_hbm, vg_hbm, out_ref, out_sem,
):
    count = q_ref.shape[0] // CHUNK
    stores = []
    for c in range(count):
        rows = pl.ds(c * CHUNK, CHUNK)
        kv_used = (entering[0] + before[c] if c else entering[0]).astype(BF16)
        back_used = (entering[1] + after[c] if c < count - 1 else entering[1]).astype(BF16)
        query, key, value, grad = (x[rows, :] for x in (q_ref, k_ref, v_ref, sg_ref))
        out_ref[0, rows, :] = (
            scale_ref[rows, :] * (acc[0, rows, :] + dot(query, kv_used))
        ).astype(BF16)
        out_ref[1, rows, :] = (acc[1, rows, :] + dot_bt(grad, kv_used)).astype(BF16)
        out_ref[2, rows, :] = (acc[2, rows, :] + dot_bt(value, back_used)).astype(BF16)
        out_ref[3, rows, :] = (acc[3, rows, :] + dot(key, back_used)).astype(BF16)
        for i, dst in enumerate((att_hbm, qg_hbm, kg_hbm, vg_hbm)):
            store = pltpu.make_async_copy(
                out_ref.at[i, rows, :], dst.at[rows, :], out_sem.at[i, c]
            )
            store.start()
            stores.append(store)
    for store in stores:
        store.wait()


def per_device(n_seq, queries, key_vectors, value_vectors, out_grad):
    rows, width = queries.shape
    count = rows // CHUNK
    n_sem = n_seq + 1
    args = [
        pltpu.with_memory_space_constraint(x, pltpu.HBM)
        for x in (queries, key_vectors, value_vectors, out_grad)
    ]
    tokens = pltpu.VMEM((rows, width), BF16)
    held = [
        ((rows, width), BF16),
        ((rows, width), BF16),
        ((rows, width), BF16),
        ((rows, width), BF16),
        ((rows, width), F32),
        ((4, rows, width), F32),
        ((count, width, width), F32),
        ((count, width, width), F32),
        ((2, width, width), F32),
    ]
    in_vmem = pl.BlockSpec(memory_space=pltpu.VMEM)
    in_hbm = pl.BlockSpec(memory_space=pltpu.HBM)
    local = pl.pallas_call(
        functools.partial(exchange_kernel, n_seq),
        out_shape=[pltpu.VMEM(shape, kind) for shape, kind in held],
        in_specs=[in_hbm] * 4,
        out_specs=[in_vmem] * len(held),
        scratch_shapes=[
            tokens,
            pltpu.VMEM((2, width, width), F32),
            pltpu.VMEM((width, width), F32),
            pltpu.VMEM((width, width), F32),
            pltpu.VMEM((n_seq - 1, width, width), F32),
            pltpu.VMEM((width, width), F32),
            pltpu.VMEM((width, width), F32),
            pltpu.SemaphoreType.DMA((4,)),
            pltpu.SemaphoreType.DMA((n_sem,)),
            pltpu.SemaphoreType.DMA((n_sem,)),
        ],
        compiler_params=pltpu.CompilerParams(
            collective_id=0, has_side_effects=True, vmem_limit_bytes=24 * 2**20
        ),
        name="exchange",
    )(*args)
    return pl.pallas_call(
        carried_kernel,
        out_shape=[pltpu.HBM((rows, width), BF16)] * 4,
        in_specs=[in_vmem] * len(held),
        out_specs=[in_hbm] * 4,
        scratch_shapes=[
            pltpu.VMEM((4, rows, width), BF16),
            pltpu.SemaphoreType.DMA((4, count)),
        ],
        compiler_params=pltpu.CompilerParams(vmem_limit_bytes=24 * 2**20),
        name="carried",
    )(*(pltpu.with_memory_space_constraint(x, pltpu.VMEM) for x in local))


def solution(mesh):
    spec = P("seq", "inner")
    return jax.shard_map(
        functools.partial(per_device, mesh.shape["seq"]),
        mesh=mesh,
        in_specs=(spec,) * 4,
        out_specs=(spec,) * 4,
        check_vma=False,
    )
```

```python
import functools

import jax
import jax.numpy as jnp
from jax import lax
from jax.experimental import pallas as pl
from jax.experimental.pallas import tpu as pltpu
from jax.sharding import PartitionSpec as P

MESH = pl.DeviceIdType.MESH
CHUNK = 256
F32 = jnp.float32
BF16 = jnp.bfloat16


def dot(a, b):
    return lax.dot_general(a, b, (((1,), (0,)), ((), ())), preferred_element_type=F32)


def dot_bt(a, b):
    return lax.dot_general(a, b, (((1,), (1,)), ((), ())), preferred_element_type=F32)


def xor(index, mask):
    bit = 1
    out = index
    while bit <= mask:
        if mask & bit:
            out = out + bit - 2 * bit * ((index // bit) % 2)
        bit *= 2
    return out


def exchange_kernel(
    n_seq,
    q_hbm, k_hbm, v_hbm, o_hbm,
    q_ref, k_ref, v_ref, sg_ref, scale_ref, acc, before, after, entering,
    o_ref, own, part, mid, got, ship, land,
    in_sem, send_sem, recv_sem,
):
    rows, width = q_ref.shape
    count = rows // CHUNK
    seq = lax.axis_index("seq")
    side = lax.axis_index("inner") % 2
    partner = {"inner": lax.axis_index("inner") + 1 - 2 * side}
    masks = sorted(range(1, n_seq), key=lambda m: -bin(m).count("1"))

    loads = [
        pltpu.make_async_copy(src, dst, in_sem.at[i])
        for i, (src, dst) in enumerate(
            ((o_hbm, o_ref), (q_hbm, q_ref), (k_hbm, k_ref), (v_hbm, v_ref))
        )
    ]
    for load in loads:
        load.start()

    barrier = pltpu.get_barrier_semaphore()
    pl.semaphore_signal(barrier, inc=1, device_id=partner, device_id_type=MESH)
    for mask in masks:
        pl.semaphore_signal(
            barrier, inc=1, device_id={"seq": xor(seq, mask)}, device_id_type=MESH
        )

    def chunk(c):
        return pl.ds(c * CHUNK, CHUNK)

    to_partner = pltpu.make_async_remote_copy(
        own.at[1 - side], part, send_sem.at[0], recv_sem.at[0],
        device_id=partner, device_id_type=MESH,
    )
    to_peers = []
    for i, mask in enumerate(masks):
        earlier = (seq // (1 << (mask.bit_length() - 1))) % 2
        copy = pltpu.make_async_remote_copy(
            mid, got.at[i], send_sem.at[2 + i], recv_sem.at[2 + i],
            device_id={"seq": xor(seq, mask)}, device_id_type=MESH,
        )
        to_peers.append((earlier, copy))
    finished = pltpu.make_async_remote_copy(
        ship, land, send_sem.at[1], recv_sem.at[1],
        device_id=partner, device_id_type=MESH,
    )

    base = (seq * 2 + side) * rows
    for c in range(count):
        place = lax.broadcasted_iota(jnp.int32, (CHUNK, width), 0) + (base + c * CHUNK)
        scale_ref[chunk(c), :] = lax.rsqrt(width * (place.astype(F32) + 1.0))

    eye = (
        lax.broadcasted_iota(jnp.int32, (width, width), 0)
        == lax.broadcasted_iota(jnp.int32, (width, width), 1)
    ).astype(F32).astype(BF16)

    def flip(a):
        return dot_bt(eye, a).astype(BF16)

    row_ids = lax.broadcasted_iota(jnp.int32, (CHUNK, CHUNK), 0)
    column_ids = lax.broadcasted_iota(jnp.int32, (CHUNK, CHUNK), 1)
    causal, causal_t = row_ids >= column_ids, row_ids <= column_ids

    def local(c):
        query, key = q_ref[chunk(c), :], k_ref[chunk(c), :]
        value, grad = v_ref[chunk(c), :], sg_ref[chunk(c), :]
        weights = jnp.where(causal, dot_bt(query, key), 0.0).astype(BF16)
        acc[0, chunk(c), :] = dot(weights, value)
        grad_scores = jnp.where(causal, dot_bt(grad, value), 0.0).astype(BF16)
        acc[1, chunk(c), :] = dot(grad_scores, key)
        grad_scores_t = jnp.where(causal_t, dot_bt(value, grad), 0.0).astype(BF16)
        acc[2, chunk(c), :] = dot(grad_scores_t, query)
        weights_t = jnp.where(causal_t, dot_bt(key, query), 0.0).astype(BF16)
        acc[3, chunk(c), :] = dot(weights_t, grad)

    loads[0].wait()
    loads[1].wait()
    total = None
    for c in reversed(range(count)):
        scaled = (scale_ref[chunk(c), :] * o_ref[chunk(c), :].astype(F32)).astype(BF16)
        sg_ref[chunk(c), :] = scaled
        outer = dot(flip(q_ref[chunk(c), :]), scaled)
        after[c] = jnp.zeros_like(outer) if total is None else total
        total = outer if total is None else total + outer
    own[1] = total

    @pl.when(seq != 0)
    def _():
        pl.semaphore_wait(barrier, n_seq)
        pl.when(side == 0)(to_partner.start)

    loads[2].wait()
    loads[3].wait()
    total = None
    for c in range(count):
        outer = dot(flip(k_ref[chunk(c), :]), v_ref[chunk(c), :])
        before[c] = jnp.zeros_like(outer) if total is None else total
        total = outer if total is None else total + outer
    own[0] = total

    ahead = count // 2

    @pl.when(seq == 0)
    def _():
        for c in range(ahead):
            local(c)

    @pl.when(seq == 0)
    def _():
        pl.semaphore_wait(barrier, n_seq)
        pl.when(side == 0)(to_partner.start)

    pl.when(side == 1)(to_partner.start)

    def send_sum(kind):
        to_partner.wait_recv()
        mid[...] = own[kind] + part[...]
        for earlier, copy in to_peers:
            pl.when(earlier == kind)(copy.start)

    pl.when(side == 1)(lambda: send_sum(1))

    @pl.when(seq != 0)
    def _():
        local(0)

    pl.when(side == 0)(lambda: send_sum(0))

    @pl.when(seq != 0)
    def _():
        for c in range(1, ahead):
            local(c)

    for c in range(ahead, count):
        local(c)

    entering[side] = jnp.zeros((width, width), F32)
    for i in reversed(range(len(to_peers))):
        earlier, copy = to_peers[i]

        @pl.when(earlier != side)
        def _():
            copy.wait_recv()
            entering[side] += got[i]

    ship[...] = entering[side] + own[side]
    finished.start()
    finished.wait_recv()
    entering[1 - side] = land[...]

    to_partner.wait_send()
    for earlier, copy in to_peers:
        pl.when(earlier == side)(copy.wait_send)
    finished.wait_send()


def carried_kernel(
    q_ref, k_ref, v_ref, sg_ref, scale_ref, acc, before, after, entering,
    att_hbm, qg_hbm, kg_hbm, vg_hbm, out_ref, out_sem,
):
    count = q_ref.shape[0] // CHUNK
    stores = []
    for c in range(count):
        rows = pl.ds(c * CHUNK, CHUNK)
        kv_used = (entering[0] + before[c] if c else entering[0]).astype(BF16)
        back_used = (entering[1] + after[c] if c < count - 1 else entering[1]).astype(BF16)
        query, key, value, grad = (x[rows, :] for x in (q_ref, k_ref, v_ref, sg_ref))
        out_ref[0, rows, :] = (
            scale_ref[rows, :] * (acc[0, rows, :] + dot(query, kv_used))
        ).astype(BF16)
        out_ref[1, rows, :] = (acc[1, rows, :] + dot_bt(grad, kv_used)).astype(BF16)
        out_ref[2, rows, :] = (acc[2, rows, :] + dot_bt(value, back_used)).astype(BF16)
        out_ref[3, rows, :] = (acc[3, rows, :] + dot(key, back_used)).astype(BF16)
        for i, dst in enumerate((att_hbm, qg_hbm, kg_hbm, vg_hbm)):
            store = pltpu.make_async_copy(
                out_ref.at[i, rows, :], dst.at[rows, :], out_sem.at[i, c]
            )
            store.start()
            stores.append(store)
    for store in stores:
        store.wait()


def per_device(n_seq, queries, key_vectors, value_vectors, out_grad):
    rows, width = queries.shape
    count = rows // CHUNK
    n_sem = n_seq + 1
    args = [
        pltpu.with_memory_space_constraint(x, pltpu.HBM)
        for x in (queries, key_vectors, value_vectors, out_grad)
    ]
    tokens = pltpu.VMEM((rows, width), BF16)
    held = [
        ((rows, width), BF16),
        ((rows, width), BF16),
        ((rows, width), BF16),
        ((rows, width), BF16),
        ((rows, width), F32),
        ((4, rows, width), F32),
        ((count, width, width), F32),
        ((count, width, width), F32),
        ((2, width, width), F32),
    ]
    in_vmem = pl.BlockSpec(memory_space=pltpu.VMEM)
    in_hbm = pl.BlockSpec(memory_space=pltpu.HBM)
    local = pl.pallas_call(
        functools.partial(exchange_kernel, n_seq),
        out_shape=[pltpu.VMEM(shape, kind) for shape, kind in held],
        in_specs=[in_hbm] * 4,
        out_specs=[in_vmem] * len(held),
        scratch_shapes=[
            tokens,
            pltpu.VMEM((2, width, width), F32),
            pltpu.VMEM((width, width), F32),
            pltpu.VMEM((width, width), F32),
            pltpu.VMEM((n_seq - 1, width, width), F32),
            pltpu.VMEM((width, width), F32),
            pltpu.VMEM((width, width), F32),
            pltpu.SemaphoreType.DMA((4,)),
            pltpu.SemaphoreType.DMA((n_sem,)),
            pltpu.SemaphoreType.DMA((n_sem,)),
        ],
        compiler_params=pltpu.CompilerParams(
            collective_id=0, has_side_effects=True, vmem_limit_bytes=24 * 2**20
        ),
        name="exchange",
    )(*args)
    return pl.pallas_call(
        carried_kernel,
        out_shape=[pltpu.HBM((rows, width), BF16)] * 4,
        in_specs=[in_vmem] * len(held),
        out_specs=[in_hbm] * 4,
        scratch_shapes=[
            pltpu.VMEM((4, rows, width), BF16),
            pltpu.SemaphoreType.DMA((4, count)),
        ],
        compiler_params=pltpu.CompilerParams(vmem_limit_bytes=24 * 2**20),
        name="carried",
    )(*(pltpu.with_memory_space_constraint(x, pltpu.VMEM) for x in local))


def solution(mesh):
    spec = P("seq", "inner")
    return jax.shard_map(
        functools.partial(per_device, mesh.shape["seq"]),
        mesh=mesh,
        in_specs=(spec,) * 4,
        out_specs=(spec,) * 4,
        check_vma=False,
    )
```

```python
import functools

import jax
import jax.numpy as jnp
from jax import lax
from jax.experimental import pallas as pl
from jax.experimental.pallas import tpu as pltpu
from jax.sharding import PartitionSpec as P

MESH = pl.DeviceIdType.MESH
CHUNK = 256
F32 = jnp.float32
BF16 = jnp.bfloat16


def dot(a, b):
    return lax.dot_general(a, b, (((1,), (0,)), ((), ())), preferred_element_type=F32)


def dot_bt(a, b):
    return lax.dot_general(a, b, (((1,), (1,)), ((), ())), preferred_element_type=F32)


def dot_at(a, b):
    return lax.dot_general(a, b, (((0,), (0,)), ((), ())), preferred_element_type=F32)


def xor(index, mask):
    bit = 1
    out = index
    while bit <= mask:
        if mask & bit:
            out = out + bit - 2 * bit * ((index // bit) % 2)
        bit *= 2
    return out


def exchange_kernel(
    n_seq,
    q_hbm, k_hbm, v_hbm, o_hbm,
    q_ref, k_ref, v_ref, sg_ref, scale_ref, acc, before, after, entering,
    o_ref, own, part, mid, got, ship, land,
    in_sem, send_sem, recv_sem,
):
    rows, width = q_ref.shape
    count = rows // CHUNK
    seq = lax.axis_index("seq")
    side = lax.axis_index("inner") % 2
    partner = {"inner": lax.axis_index("inner") + 1 - 2 * side}
    masks = sorted(range(1, n_seq), key=lambda m: -bin(m).count("1"))

    loads = [
        pltpu.make_async_copy(src, dst, in_sem.at[i])
        for i, (src, dst) in enumerate(
            ((o_hbm, o_ref), (q_hbm, q_ref), (k_hbm, k_ref), (v_hbm, v_ref))
        )
    ]
    for load in loads:
        load.start()

    barrier = pltpu.get_barrier_semaphore()
    pl.semaphore_signal(barrier, inc=1, device_id=partner, device_id_type=MESH)
    for mask in masks:
        pl.semaphore_signal(
            barrier, inc=1, device_id={"seq": xor(seq, mask)}, device_id_type=MESH
        )

    def chunk(c):
        return pl.ds(pl.multiple_of(c * CHUNK, CHUNK), CHUNK)

    to_partner = pltpu.make_async_remote_copy(
        own.at[1 - side], part, send_sem.at[0], recv_sem.at[0],
        device_id=partner, device_id_type=MESH,
    )
    to_peers = []
    for i, mask in enumerate(masks):
        earlier = (seq // (1 << (mask.bit_length() - 1))) % 2
        copy = pltpu.make_async_remote_copy(
            mid, got.at[i], send_sem.at[2 + i], recv_sem.at[2 + i],
            device_id={"seq": xor(seq, mask)}, device_id_type=MESH,
        )
        to_peers.append((earlier, copy))
    finished = pltpu.make_async_remote_copy(
        ship, land, send_sem.at[1], recv_sem.at[1],
        device_id=partner, device_id_type=MESH,
    )

    base = (seq * 2 + side) * rows
    @pl.loop(0, count)
    def _(c):
        place = lax.broadcasted_iota(jnp.int32, (CHUNK, width), 0) + (base + c * CHUNK)
        scale_ref[chunk(c), :] = lax.rsqrt(width * (place.astype(F32) + 1.0))

    loads[0].wait()
    loads[1].wait()
    own[...] = jnp.zeros(own.shape, F32)

    @pl.loop(0, count)
    def _(step):
        c = count - 1 - step
        scaled = (scale_ref[chunk(c), :] * o_ref[chunk(c), :].astype(F32)).astype(BF16)
        sg_ref[chunk(c), :] = scaled
        after[c] = own[1]
        own[1] += dot_at(q_ref[chunk(c), :], scaled)

    @pl.when(seq == n_seq - 1)
    def _():
        pl.semaphore_wait(barrier, n_seq)
        pl.when(side == 0)(to_partner.start)

    loads[2].wait()
    loads[3].wait()

    @pl.loop(0, count)
    def _(c):
        before[c] = own[0]
        own[0] += dot_at(k_ref[chunk(c), :], v_ref[chunk(c), :])

    @pl.when(seq != n_seq - 1)
    def _():
        pl.semaphore_wait(barrier, n_seq)
        pl.when(side == 0)(to_partner.start)

    pl.when(side == 1)(to_partner.start)

    causal = lax.broadcasted_iota(jnp.int32, (CHUNK, CHUNK), 0) >= lax.broadcasted_iota(
        jnp.int32, (CHUNK, CHUNK), 1
    )

    def local(c):
        query, key = q_ref[chunk(c), :], k_ref[chunk(c), :]
        value, grad = v_ref[chunk(c), :], sg_ref[chunk(c), :]
        weights = jnp.where(causal, dot_bt(query, key), 0.0).astype(BF16)
        grad_scores = jnp.where(causal, dot_bt(grad, value), 0.0).astype(BF16)
        acc[0, chunk(c), :] = dot(weights, value)
        acc[1, chunk(c), :] = dot(grad_scores, key)
        acc[2, chunk(c), :] = dot_at(grad_scores, query)
        acc[3, chunk(c), :] = dot_at(weights, grad)

    def send_sum(kind):
        to_partner.wait_recv()
        mid[...] = own[kind] + part[...]
        for earlier, copy in to_peers:
            pl.when(earlier == kind)(copy.start)

    pl.when(side == 1)(lambda: send_sum(1))
    pl.when(side == 0)(lambda: send_sum(0))
    pl.loop(0, count)(local)

    entering[side] = jnp.zeros((width, width), F32)
    for i in reversed(range(len(to_peers))):
        earlier, copy = to_peers[i]

        @pl.when(earlier != side)
        def _():
            copy.wait_recv()
            entering[side] += got[i]

    ship[...] = entering[side] + own[side]
    finished.start()
    finished.wait_recv()
    entering[1 - side] = land[...]

    to_partner.wait_send()
    for earlier, copy in to_peers:
        pl.when(earlier == side)(copy.wait_send)
    finished.wait_send()


def carried_kernel(
    q_ref, k_ref, v_ref, sg_ref, scale_ref, acc, before, after, entering,
    att_hbm, qg_hbm, kg_hbm, vg_hbm, out_ref, out_sem,
):
    count = q_ref.shape[0] // CHUNK
    outs = (att_hbm, qg_hbm, kg_hbm, vg_hbm)

    @pl.loop(0, count)
    def _(c):
        rows = pl.ds(pl.multiple_of(c * CHUNK, CHUNK), CHUNK)
        kv_used = (entering[0] + before[c]).astype(BF16)
        back_used = (entering[1] + after[c]).astype(BF16)
        query, key, value, grad = (x[rows, :] for x in (q_ref, k_ref, v_ref, sg_ref))
        out_ref[0, rows, :] = (
            scale_ref[rows, :] * (acc[0, rows, :] + dot(query, kv_used))
        ).astype(BF16)
        out_ref[1, rows, :] = (acc[1, rows, :] + dot_bt(grad, kv_used)).astype(BF16)
        out_ref[2, rows, :] = (acc[2, rows, :] + dot_bt(value, back_used)).astype(BF16)
        out_ref[3, rows, :] = (acc[3, rows, :] + dot(key, back_used)).astype(BF16)
        for i, dst in enumerate(outs):
            pltpu.make_async_copy(
                out_ref.at[i, rows, :], dst.at[rows, :], out_sem.at[i]
            ).start()

    for i, dst in enumerate(outs):
        pltpu.make_async_copy(out_ref.at[i], dst, out_sem.at[i]).wait()


def per_device(n_seq, queries, key_vectors, value_vectors, out_grad):
    rows, width = queries.shape
    count = rows // CHUNK
    n_sem = n_seq + 1
    args = [
        pltpu.with_memory_space_constraint(x, pltpu.HBM)
        for x in (queries, key_vectors, value_vectors, out_grad)
    ]
    tokens = pltpu.VMEM((rows, width), BF16)
    held = [
        ((rows, width), BF16),
        ((rows, width), BF16),
        ((rows, width), BF16),
        ((rows, width), BF16),
        ((rows, width), F32),
        ((4, rows, width), F32),
        ((count, width, width), F32),
        ((count, width, width), F32),
        ((2, width, width), F32),
    ]
    in_vmem = pl.BlockSpec(memory_space=pltpu.VMEM)
    in_hbm = pl.BlockSpec(memory_space=pltpu.HBM)
    local = pl.pallas_call(
        functools.partial(exchange_kernel, n_seq),
        out_shape=[pltpu.VMEM(shape, kind) for shape, kind in held],
        in_specs=[in_hbm] * 4,
        out_specs=[in_vmem] * len(held),
        scratch_shapes=[
            tokens,
            pltpu.VMEM((2, width, width), F32),
            pltpu.VMEM((width, width), F32),
            pltpu.VMEM((width, width), F32),
            pltpu.VMEM((n_seq - 1, width, width), F32),
            pltpu.VMEM((width, width), F32),
            pltpu.VMEM((width, width), F32),
            pltpu.SemaphoreType.DMA((4,)),
            pltpu.SemaphoreType.DMA((n_sem,)),
            pltpu.SemaphoreType.DMA((n_sem,)),
        ],
        compiler_params=pltpu.CompilerParams(
            collective_id=0, has_side_effects=True, vmem_limit_bytes=24 * 2**20
        ),
        name="exchange",
    )(*args)
    return pl.pallas_call(
        carried_kernel,
        out_shape=[pltpu.HBM((rows, width), BF16)] * 4,
        in_specs=[in_vmem] * len(held),
        out_specs=[in_hbm] * 4,
        scratch_shapes=[
            pltpu.VMEM((4, rows, width), BF16),
            pltpu.SemaphoreType.DMA((4,)),
        ],
        compiler_params=pltpu.CompilerParams(vmem_limit_bytes=24 * 2**20),
        name="carried",
    )(*(pltpu.with_memory_space_constraint(x, pltpu.VMEM) for x in local))


def solution(mesh):
    spec = P("seq", "inner")
    return jax.shard_map(
        functools.partial(per_device, mesh.shape["seq"]),
        mesh=mesh,
        in_specs=(spec,) * 4,
        out_specs=(spec,) * 4,
        check_vma=False,
    )
```

```python
import functools

import jax
import jax.numpy as jnp
from jax import lax
from jax.experimental import pallas as pl
from jax.experimental.pallas import tpu as pltpu
from jax.sharding import PartitionSpec as P

MESH = pl.DeviceIdType.MESH
CHUNK = 256
F32 = jnp.float32
BF16 = jnp.bfloat16


def dot(a, b):
    return lax.dot_general(a, b, (((1,), (0,)), ((), ())), preferred_element_type=F32)


def dot_bt(a, b):
    return lax.dot_general(a, b, (((1,), (1,)), ((), ())), preferred_element_type=F32)


def dot_at(a, b):
    return lax.dot_general(a, b, (((0,), (0,)), ((), ())), preferred_element_type=F32)


def xor(index, mask):
    bit = 1
    out = index
    while bit <= mask:
        if mask & bit:
            out = out + bit - 2 * bit * ((index // bit) % 2)
        bit *= 2
    return out


def exchange_kernel(
    n_seq,
    q_hbm, k_hbm, v_hbm, o_hbm,
    q_ref, k_ref, v_ref, sg_ref, scale_ref, acc, before, after, entering,
    o_ref, own, part, mid, got, extra, ship, land,
    in_sem, send_sem, recv_sem,
):
    rows, width = q_ref.shape
    count = rows // CHUNK
    seq = lax.axis_index("seq")
    side = lax.axis_index("inner") % 2
    partner = {"inner": lax.axis_index("inner") + 1 - 2 * side}
    masks = sorted(range(1, n_seq), key=lambda m: -bin(m).count("1"))

    loads = [
        pltpu.make_async_copy(src, dst, in_sem.at[i])
        for i, (src, dst) in enumerate(
            ((o_hbm, o_ref), (q_hbm, q_ref), (k_hbm, k_ref), (v_hbm, v_ref))
        )
    ]
    for load in loads:
        load.start()

    barrier = pltpu.get_barrier_semaphore()
    pl.semaphore_signal(barrier, inc=1, device_id=partner, device_id_type=MESH)
    for mask in masks:
        pl.semaphore_signal(
            barrier, inc=1, device_id={"seq": xor(seq, mask)}, device_id_type=MESH
        )

    is_last = seq == n_seq - 1
    across = {
        "seq": xor(seq, n_seq - 1),
        "inner": lax.axis_index("inner") + 1 - 2 * side,
    }

    @pl.when((seq == 0) & (side == 1))
    def _():
        pl.semaphore_signal(barrier, inc=1, device_id=across, device_id_type=MESH)

    def chunk(c):
        return pl.ds(c * CHUNK, CHUNK)

    to_partner = pltpu.make_async_remote_copy(
        own.at[1 - side], part, send_sem.at[0], recv_sem.at[0],
        device_id=partner, device_id_type=MESH,
    )
    to_peers = []
    for i, mask in enumerate(masks):
        earlier = (seq // (1 << (mask.bit_length() - 1))) % 2
        copy = pltpu.make_async_remote_copy(
            mid, got.at[i], send_sem.at[2 + i], recv_sem.at[2 + i],
            device_id={"seq": xor(seq, mask)}, device_id_type=MESH,
        )
        to_peers.append((earlier, copy))
    direct = pltpu.make_async_remote_copy(
        own.at[1], extra, send_sem.at[1 + n_seq], recv_sem.at[1 + n_seq],
        device_id=across, device_id_type=MESH,
    )
    direct_twin = pltpu.make_async_remote_copy(
        own.at[1], got.at[0], send_sem.at[2], recv_sem.at[2],
        device_id={"seq": xor(seq, masks[0])}, device_id_type=MESH,
    )
    finished = pltpu.make_async_remote_copy(
        ship, land, send_sem.at[1], recv_sem.at[1],
        device_id=partner, device_id_type=MESH,
    )

    base = (seq * 2 + side) * rows
    for c in range(count):
        place = lax.broadcasted_iota(jnp.int32, (CHUNK, width), 0) + (base + c * CHUNK)
        scale_ref[chunk(c), :] = lax.rsqrt(width * (place.astype(F32) + 1.0))

    row_ids = lax.broadcasted_iota(jnp.int32, (CHUNK, CHUNK), 0)
    column_ids = lax.broadcasted_iota(jnp.int32, (CHUNK, CHUNK), 1)
    causal, causal_t = row_ids >= column_ids, row_ids <= column_ids

    def local(c):
        query, key = q_ref[chunk(c), :], k_ref[chunk(c), :]
        value, grad = v_ref[chunk(c), :], sg_ref[chunk(c), :]
        weights = jnp.where(causal, dot_bt(query, key), 0.0).astype(BF16)
        acc[0, chunk(c), :] = dot(weights, value)
        grad_scores = jnp.where(causal, dot_bt(grad, value), 0.0).astype(BF16)
        acc[1, chunk(c), :] = dot(grad_scores, key)
        grad_scores_t = jnp.where(causal_t, dot_bt(value, grad), 0.0).astype(BF16)
        acc[2, chunk(c), :] = dot(grad_scores_t, query)
        weights_t = jnp.where(causal_t, dot_bt(key, query), 0.0).astype(BF16)
        acc[3, chunk(c), :] = dot(weights_t, grad)

    loads[0].wait()
    loads[1].wait()
    total = None
    for c in reversed(range(count)):
        scaled = (scale_ref[chunk(c), :] * o_ref[chunk(c), :].astype(F32)).astype(BF16)
        sg_ref[chunk(c), :] = scaled
        outer = dot_at(q_ref[chunk(c), :], scaled)
        after[c] = jnp.zeros_like(outer) if total is None else total
        total = outer if total is None else total + outer
    own[1] = total

    @pl.when(is_last)
    def _():
        pl.semaphore_wait(barrier, n_seq + 1 - side)
        pl.when(side == 0)(direct.start)
        pl.when(side == 1)(direct_twin.start)
        pl.when(side == 0)(to_partner.start)

    loads[2].wait()
    loads[3].wait()
    total = None
    for c in range(count):
        outer = dot_at(k_ref[chunk(c), :], v_ref[chunk(c), :])
        before[c] = jnp.zeros_like(outer) if total is None else total
        total = outer if total is None else total + outer
    own[0] = total

    ahead = count // 2

    @pl.when(seq == 0)
    def _():
        for c in range(ahead):
            local(c)

    @pl.when(seq != n_seq - 1)
    def _():
        pl.semaphore_wait(barrier, n_seq)
        pl.when(side == 0)(to_partner.start)

    pl.when(side == 1)(to_partner.start)

    def send_sum(kind):
        to_partner.wait_recv()
        mid[...] = own[kind] + part[...]
        for i, (earlier, copy) in enumerate(to_peers):
            if i == 0:
                pl.when((earlier == kind) & (seq != n_seq - 1))(copy.start)
            else:
                pl.when(earlier == kind)(copy.start)

    pl.when(side == 1)(lambda: send_sum(1))

    @pl.when(seq != 0)
    def _():
        local(0)

    pl.when(side == 0)(lambda: send_sum(0))

    @pl.when(seq != 0)
    def _():
        for c in range(1, ahead):
            local(c)

    for c in range(ahead, count):
        local(c)

    entering[side] = jnp.zeros((width, width), F32)
    for i in reversed(range(len(to_peers))):
        earlier, copy = to_peers[i]

        @pl.when(earlier != side)
        def _():
            copy.wait_recv()
            entering[side] += got[i]

    @pl.when((seq == 0) & (side == 1))
    def _():
        direct.wait_recv()
        entering[1] += extra[...]

    ship[...] = entering[side] + own[side]
    finished.start()
    finished.wait_recv()
    entering[1 - side] = land[...]

    to_partner.wait_send()
    pl.when(is_last & (side == 0))(direct.wait_send)
    for earlier, copy in to_peers:
        pl.when(earlier == side)(copy.wait_send)
    finished.wait_send()


def carried_kernel(
    q_ref, k_ref, v_ref, sg_ref, scale_ref, acc, before, after, entering,
    att_hbm, qg_hbm, kg_hbm, vg_hbm, out_ref, out_sem,
):
    count = q_ref.shape[0] // CHUNK
    stores = []
    for c in range(count):
        rows = pl.ds(c * CHUNK, CHUNK)
        kv_used = (entering[0] + before[c] if c else entering[0]).astype(BF16)
        back_used = (entering[1] + after[c] if c < count - 1 else entering[1]).astype(BF16)
        query, key, value, grad = (x[rows, :] for x in (q_ref, k_ref, v_ref, sg_ref))
        out_ref[0, rows, :] = (
            scale_ref[rows, :] * (acc[0, rows, :] + dot(query, kv_used))
        ).astype(BF16)
        out_ref[1, rows, :] = (acc[1, rows, :] + dot_bt(grad, kv_used)).astype(BF16)
        out_ref[2, rows, :] = (acc[2, rows, :] + dot_bt(value, back_used)).astype(BF16)
        out_ref[3, rows, :] = (acc[3, rows, :] + dot(key, back_used)).astype(BF16)
        for i, dst in enumerate((att_hbm, qg_hbm, kg_hbm, vg_hbm)):
            store = pltpu.make_async_copy(
                out_ref.at[i, rows, :], dst.at[rows, :], out_sem.at[i, c]
            )
            store.start()
            stores.append(store)
    for store in stores:
        store.wait()


def per_device(n_seq, queries, key_vectors, value_vectors, out_grad):
    rows, width = queries.shape
    count = rows // CHUNK
    n_sem = n_seq + 2
    args = [
        pltpu.with_memory_space_constraint(x, pltpu.HBM)
        for x in (queries, key_vectors, value_vectors, out_grad)
    ]
    tokens = pltpu.VMEM((rows, width), BF16)
    held = [
        ((rows, width), BF16),
        ((rows, width), BF16),
        ((rows, width), BF16),
        ((rows, width), BF16),
        ((rows, width), F32),
        ((4, rows, width), F32),
        ((count, width, width), F32),
        ((count, width, width), F32),
        ((2, width, width), F32),
    ]
    in_vmem = pl.BlockSpec(memory_space=pltpu.VMEM)
    in_hbm = pl.BlockSpec(memory_space=pltpu.HBM)
    local = pl.pallas_call(
        functools.partial(exchange_kernel, n_seq),
        out_shape=[pltpu.VMEM(shape, kind) for shape, kind in held],
        in_specs=[in_hbm] * 4,
        out_specs=[in_vmem] * len(held),
        scratch_shapes=[
            tokens,
            pltpu.VMEM((2, width, width), F32),
            pltpu.VMEM((width, width), F32),
            pltpu.VMEM((width, width), F32),
            pltpu.VMEM((n_seq - 1, width, width), F32),
            pltpu.VMEM((width, width), F32),
            pltpu.VMEM((width, width), F32),
            pltpu.VMEM((width, width), F32),
            pltpu.SemaphoreType.DMA((4,)),
            pltpu.SemaphoreType.DMA((n_sem,)),
            pltpu.SemaphoreType.DMA((n_sem,)),
        ],
        compiler_params=pltpu.CompilerParams(
            collective_id=0, has_side_effects=True, vmem_limit_bytes=24 * 2**20
        ),
        name="exchange",
    )(*args)
    return pl.pallas_call(
        carried_kernel,
        out_shape=[pltpu.HBM((rows, width), BF16)] * 4,
        in_specs=[in_vmem] * len(held),
        out_specs=[in_hbm] * 4,
        scratch_shapes=[
            pltpu.VMEM((4, rows, width), BF16),
            pltpu.SemaphoreType.DMA((4, count)),
        ],
        compiler_params=pltpu.CompilerParams(vmem_limit_bytes=24 * 2**20),
        name="carried",
    )(*(pltpu.with_memory_space_constraint(x, pltpu.VMEM) for x in local))


def solution(mesh):
    spec = P("seq", "inner")
    return jax.shard_map(
        functools.partial(per_device, mesh.shape["seq"]),
        mesh=mesh,
        in_specs=(spec,) * 4,
        out_specs=(spec,) * 4,
        check_vma=False,
    )
```
